512 devices in a mesh: dp: 32 (over z, y_hi), seq: 16 (over x, y_lo, core).
Axes of the slice: x: 4, y: 8 (y_hi: 4, y_lo: 2; y = y_hi * 2 + y_lo), z: 8, core: 2. Of those that a mesh axis runs over, the one named last changes fastest.
Arguments:
- latents: bfloat16 [32, 16, 128, 1152], P('dp', 'seq'), may hold values from -6 to 6
- targets: bfloat16 [32, 16, 128, 1152], P('dp', 'seq'), may hold values from -6 to 6
- modulation: float32 [32, 2, 3, 1152], P('dp'), may hold values from -3 to 3
- query_key_value_weight: bfloat16 [2, 1152, 1728], P(None, 'dp'), may hold values from -0.1875 to 0.1875
- output_projection_weight: bfloat16 [2, 576, 1152], P(None, 'dp'), may hold values from -0.25 to 0.25
- adapter_down_weight: float32 [2, 1152, 64], replicated, may hold values from -0.1875 to 0.1875
- adapter_up_weight: float32 [2, 64, 1728], replicated, may hold values from -0.75 to 0.75
Outputs:
- grad_down: float32 [2, 1152, 64], replicated
- grad_up: float32 [2, 64, 1728], replicated
The draws below stay inside these ranges and needn't reach their ends.
All inputs are finite; a program needn't handle non-finite values.
Results may differ from the reference program's by a relative error of at most 0.0027.
Values may be sent and summed in bfloat16 or wider, within the bound.
No kernel may reach another device: no remote copies, remote signals or barrier semaphores. Data moves between devices by JAX's collectives and lax.ppermute only.
A program may use at most 128 MiB of HBM per device.

```python
import math
import jax
import jax.numpy as jnp
from jax import lax

MODEL_WIDTH = 1152
HEADS = 8
HEAD = 72
ADAPTER_RANK = 64
S = 128
HEAD_FEATURES = 576
FRAMES = 16
CLIPS = 32


def levels(stream_key, dims, pieces, least, high):
    def one(dim, blocks):
        steps = jax.random.uniform(jax.random.fold_in(jax.random.fold_in(stream_key, 6), dim), (blocks,), jnp.float32, least / len(pieces), high / len(pieces))
        return jnp.repeat(jnp.exp(steps), dims[dim] // blocks).reshape((-1,) + (1,) * (len(dims) - dim - 1))

    factor_of = one(*pieces[0])
    for cut in pieces[1:]:
        factor_of = factor_of * one(*cut)
    return factor_of


def gaussian(rng, dims, scale, bound, shards=(), dtype=jnp.bfloat16):
    values = jax.random.normal(rng, dims, jnp.float32) * scale
    if len(shards) > 0:
        values = levels(rng, dims, shards, -0.22, 0.18) * values
    return jnp.clip(values, min=-bound, max=bound).astype(dtype)


def setup_inputs(seed: int = 0) -> dict:
    splits = jax.random.split(jax.random.key(seed), 8)
    return {
        "latents": gaussian(splits[0], (CLIPS, FRAMES, S, MODEL_WIDTH), 1.0, 6.0, ((0, 32), (1, 16))),
        "targets": gaussian(splits[1], (CLIPS, FRAMES, S, MODEL_WIDTH), 1.0, 6.0, ((0, 32), (1, 16))),
        "modulation": gaussian(splits[2], (CLIPS, 2, 3, MODEL_WIDTH), 0.5, 3.0, ((0, 32),), jnp.float32),
        "query_key_value_weight": gaussian(splits[3], (2, MODEL_WIDTH, 3 * HEAD_FEATURES), MODEL_WIDTH ** -0.5, 0.1875, ((1, 32),)),
        "output_projection_weight": gaussian(splits[4], (2, HEAD_FEATURES, MODEL_WIDTH), HEAD_FEATURES ** -0.5, 0.25, ((1, 32),)),
        "adapter_down_weight": gaussian(splits[5], (2, MODEL_WIDTH, ADAPTER_RANK), MODEL_WIDTH ** -0.5, 0.1875, (), jnp.float32),
        "adapter_up_weight": gaussian(splits[6], (2, ADAPTER_RANK, 3 * HEAD_FEATURES), ADAPTER_RANK ** -0.5, 0.75, (), jnp.float32),
    }


def layer_norm(values):
    average = lax.optimization_barrier(jnp.mean(values, -1, keepdims=True))
    centred = values - average
    spread = lax.optimization_barrier(jnp.mean(centred * centred, -1, keepdims=True))
    return centred * lax.rsqrt(spread + 1e-06)

def head_norm(values):
    return values * lax.rsqrt(lax.optimization_barrier(jnp.mean(values * values, -1, keepdims=True)) + 1e-06)

def rotary(values, count):
    half_head = HEAD // 2
    position = jnp.arange(count).astype(jnp.float32)
    frequency = jnp.exp(jnp.arange(half_head).astype(jnp.float32) * (-2.0 * math.log(10000.0) / HEAD))
    angles = position[:, None] * frequency[None, :]
    cosine = jnp.cos(angles)[:, None, None, :]
    sine_part = jnp.sin(angles)[:, None, None, :]
    first = values[..., :half_head]
    second = values[..., half_head:]
    return jnp.concatenate([first * cosine - second * sine_part, second * cosine + first * sine_part], -1)

def rounded(values):
    return lax.optimization_barrier(values.astype(jnp.bfloat16)).astype(jnp.float32)

def block(hidden, apply_modulation, query_key_value_weight, output_projection_weight, low_down, low_up, temporal_block):
    in_shape = hidden.shape
    normed = layer_norm(hidden.reshape(-1, MODEL_WIDTH).astype(jnp.float32))
    modded = (normed * (1.0 + apply_modulation[1]) + apply_modulation[0]).astype(jnp.bfloat16)
    frozen_part = jnp.dot(modded, query_key_value_weight, preferred_element_type=jnp.float32)
    reduced = jnp.dot(modded.astype(jnp.float32), low_down, precision=lax.Precision.HIGHEST)
    projected = frozen_part + jnp.dot(reduced, low_up, precision=lax.Precision.HIGHEST)
    projected = projected.reshape(in_shape[0], in_shape[1], 3, HEADS, HEAD)
    queries = head_norm(projected[:, :, 0])
    key_vecs = head_norm(projected[:, :, 1])
    if temporal_block:
        queries = rotary(queries, in_shape[0])
        key_vecs = rotary(key_vecs, in_shape[0])
    queries = rounded(queries)
    key_vecs = rounded(key_vecs)
    value_vecs = rounded(projected[:, :, 2])
    if temporal_block:
        scores = jnp.einsum('frhe,grhe->rhfg', queries, key_vecs)
    else:
        scores = jnp.einsum('fshe,fthe->fhst', queries, key_vecs)
    scores = scores * (1.0 / math.sqrt(HEAD))
    weights = jnp.exp(scores)
    weights = rounded(weights / lax.optimization_barrier(jnp.sum(weights, -1, keepdims=True)))
    if temporal_block:
        attended = jnp.einsum('rhfg,grhe->frhe', weights, value_vecs)
    else:
        attended = jnp.einsum('fhst,fthe->fshe', weights, value_vecs)
    attended = attended.astype(jnp.bfloat16).reshape(-1, HEADS * HEAD)
    mixed = jnp.dot(attended, output_projection_weight, preferred_element_type=jnp.float32)
    updated = hidden.reshape(-1, MODEL_WIDTH).astype(jnp.float32) + apply_modulation[2] * mixed
    return updated.astype(jnp.bfloat16).reshape(in_shape)

def clip_gradient_norms(latents, targets, apply_modulation, query_key_value_weight, output_projection_weight, adapter_down_weight, adapter_up_weight):

    def forward_sweep(down_pair, up_pair):
        middle_state = block(latents, apply_modulation[0], query_key_value_weight[0], output_projection_weight[0], down_pair[0], up_pair[0], False)
        return block(middle_state, apply_modulation[1], query_key_value_weight[1], output_projection_weight[1], down_pair[1], up_pair[1], True)
    produced_output, backward_sweep = jax.vjp(forward_sweep, adapter_down_weight, adapter_up_weight)
    error_grad = ((produced_output.astype(jnp.float32) - targets.astype(jnp.float32)) / MODEL_WIDTH).astype(jnp.bfloat16)
    return backward_sweep(error_grad)

def reference(latents, targets, modulation, query_key_value_weight, output_projection_weight, adapter_down_weight, adapter_up_weight):

    def one_clip(input_rows):
        return clip_gradient_norms(input_rows[0], input_rows[1], input_rows[2], query_key_value_weight, output_projection_weight, adapter_down_weight, adapter_up_weight)
    downs, ups = lax.map(one_clip, (latents, targets, modulation))
    return (lax.optimization_barrier(jnp.sum(downs, 0)), lax.optimization_barrier(jnp.sum(ups, 0)))
```

```python
import math

import jax
import jax.numpy as jnp
import numpy as np
from jax import lax
from jax.experimental import pallas as pl
from jax.experimental.pallas import tpu as pltpu
from jax.sharding import Mesh, PartitionSpec as P

WIDTH = 1152
HEADS = 8
HEAD = 72
RANK = 64
FEATURES = HEADS * HEAD
ROWS = 128
F32 = jnp.float32
BF16 = jnp.bfloat16
SCALE = 1.0 / math.sqrt(HEAD)
MIB = 1 << 20
DP = ("z", "h")
SEQ = ("x", "l", "c")


def call(kernel, out_shape, scratch=(), in_specs=None, limit=48):
    vmem = pl.BlockSpec(memory_space=pltpu.VMEM)

    def run(*operands):
        return pl.pallas_call(
            kernel,
            out_shape=out_shape,
            in_specs=in_specs or [vmem] * len(operands),
            out_specs=jax.tree.map(lambda _: vmem, out_shape),
            scratch_shapes=list(scratch),
            compiler_params=pltpu.CompilerParams(vmem_limit_bytes=limit * MIB),
        )(*operands)

    return run


def spec(space):
    return pl.BlockSpec(memory_space=space)


def dot(a, b, dims=((1,), (0,))):
    return lax.dot_general(a, b, (dims, ((), ())), preferred_element_type=F32)


NT = ((1,), (1,))
TN = ((0,), (0,))


def halves(values):
    high = values.astype(BF16)
    return high, (values - high.astype(F32)).astype(BF16)


def normalise(values):
    centred = values - jnp.mean(values, -1, keepdims=True)
    rate = lax.rsqrt(jnp.mean(centred * centred, -1, keepdims=True) + 1e-06)
    return centred * rate, rate


def lane_mask(width, dtype=F32):
    lanes = lax.broadcasted_iota(jnp.int32, (1, 128), 1)
    return (lanes < width).astype(dtype)


def split_heads(projected):
    keep = lane_mask(HEAD)
    q = projected[:, :128] * keep
    k = pltpu.roll(projected, 256 - HEAD, 1)[:, :128] * keep
    v = pltpu.roll(projected, 256 - 2 * HEAD, 1)[:, :128] * keep
    return q, k, v


def join_heads(q, k, v):
    zero = jnp.zeros_like(q)
    return (
        jnp.concatenate([q, zero], 1)
        + pltpu.roll(jnp.concatenate([k, zero], 1), HEAD, 1)
        + pltpu.roll(jnp.concatenate([v, zero], 1), 2 * HEAD, 1)
    )


def head_rate(values):
    return lax.rsqrt(jnp.sum(values * values, -1, keepdims=True) * (1.0 / HEAD) + 1e-06)


def head_norm_back(values, cotangent):
    rate = head_rate(values)
    inner = jnp.sum(cotangent * values, -1, keepdims=True) * (1.0 / HEAD)
    return rate * (cotangent - values * (rate * rate * inner))


def swap(values):
    lanes = lax.broadcasted_iota(jnp.int32, (1, 128), 1)
    return jnp.where(
        lanes < HEAD // 2,
        pltpu.roll(values, 128 - HEAD // 2, 1),
        pltpu.roll(values, HEAD // 2, 1),
    )


def softmax(scores, mask):
    weights = jnp.exp(scores * SCALE)
    if mask is not None:
        weights = weights * mask
    return weights / jnp.sum(weights, -1, keepdims=True)


def attention_back(weights, q, k, v, cotangent):
    rounded = weights.astype(BF16)
    d_v = dot(rounded, cotangent, TN).astype(BF16)
    d_weights = dot(cotangent, v, NT).astype(BF16).astype(F32)
    d_scores = weights * (d_weights - jnp.sum(d_weights * weights, -1, keepdims=True))
    d_scores = (d_scores * SCALE).astype(BF16)
    d_q = dot(d_scores, k).astype(BF16)
    d_k = dot(d_scores, q, TN).astype(BF16)
    return d_q.astype(F32), d_k.astype(F32), d_v.astype(F32)


def same_token():
    rows = lax.broadcasted_iota(jnp.int32, (ROWS, ROWS), 0)
    columns = lax.broadcasted_iota(jnp.int32, (ROWS, ROWS), 1)
    return ((rows & 7) == (columns & 7)).astype(F32)


def rotation_tables():
    row = np.arange(ROWS)
    frame = ((row // 16) % 4) * 4 + (row // 64) * 2 + (row // 8) % 2
    half = HEAD // 2
    frequency = np.exp(np.arange(half) * (-2.0 * math.log(10000.0) / HEAD))
    angle = frame[:, None] * frequency[None, :]
    cosine = np.zeros((ROWS, 128), np.float32)
    sine = np.zeros((ROWS, 128), np.float32)
    cosine[:, :half] = cosine[:, half:HEAD] = np.cos(angle)
    sine[:, :half] = -np.sin(angle)
    sine[:, half:HEAD] = np.sin(angle)
    return cosine, sine


def prologue_kernel(place, latents, modulation, qkv, out, modded, first_part, rest_part, rest):
    normed, _ = normalise(latents[...].astype(F32))
    modded[...] = (normed * (1.0 + modulation[0, 1:2]) + modulation[0, 0:1]).astype(BF16)
    rest[...] = jnp.zeros_like(rest)
    for head in range(HEADS):

        @pl.when(place[0] == head)
        def _():
            for part in range(3):
                columns = slice(part * FEATURES + head * HEAD, part * FEATURES + head * HEAD + HEAD)
                rest[0, :, part * HEAD : part * HEAD + HEAD] = qkv[0, :, columns].astype(F32)
                rest[1, :, part * HEAD : part * HEAD + HEAD] = qkv[1, :, columns].astype(F32)
            for block in range(2):
                rows = slice(18 * block, 18 * block + 18)
                rest[1, rows, 216:232] = out[block, :, 1024 + 16 * head : 1040 + 16 * head].astype(F32)
                rest[1, rows, 256:384] = out[block, :, 128 * head : 128 * head + 128].astype(F32)

    first = rest[0, :, :256].astype(BF16)
    tiles = jnp.concatenate([rest[1, :, 128 * t : 128 * t + 128] for t in range(3)], 0)
    lower, upper = tiles[:54].astype(BF16), tiles[54:].astype(BF16)
    mine = jnp.where(place[1] == 0, lower, upper)
    for copy in range(32):
        first_part[copy] = first
        rest_part[copy] = mine


def prologue(place, latents, modulation, qkv, out):
    smem, vmem = spec(pltpu.SMEM), spec(pltpu.VMEM)
    return call(
        prologue_kernel,
        (
            jax.ShapeDtypeStruct((ROWS, WIDTH), BF16),
            jax.ShapeDtypeStruct((32, 36, 256), BF16),
            jax.ShapeDtypeStruct((32, 54, 128), BF16),
        ),
        [pltpu.VMEM((2, 36, 384), F32)],
        [smem, vmem, vmem, vmem, vmem],
    )(place, latents, modulation, qkv, out)


def spatial_kernel(order, *refs):
    pieces = refs[:8]
    weight, down, up, attended, modded, projected, reduced, weights, merged, sems = refs[8:]
    copies = [
        pltpu.make_async_copy(piece, modded.at[order[i]], sems.at[i])
        for i, piece in enumerate(pieces)
    ]
    for copy in copies:
        copy.start()
    for chunk in range(32):
        merged[36 * chunk : 36 * chunk + 36, :256] = weight[chunk]
    merged[:, 256:] = down[...]
    for copy in copies:
        copy.wait()
    whole = dot(modded[...].reshape(8 * ROWS, WIDTH), merged[...])
    low = whole[:, 256:320] + whole[:, 320:384]
    high, rest = halves(low)
    reduced[...] = jnp.concatenate([high, rest], 1)
    projected[...] = whole[:, :256] + dot(jnp.concatenate([high, high, rest], 1), up[...])
    for pair in range(4):
        outs = []
        for frame in (2 * pair, 2 * pair + 1):
            q, k, v = split_heads(projected[frame * ROWS : frame * ROWS + ROWS])
            q = (q * head_rate(q)).astype(BF16)
            k = (k * head_rate(k)).astype(BF16)
            w = softmax(dot(q, k, NT), None)
            weights[frame] = w
            outs.append(dot(w.astype(BF16), v.astype(BF16)).reshape(16, 8, 128))
        rows = jnp.stack(outs, 1).reshape(16, 16, 128).astype(BF16)
        attended[:, 16 * pair : 16 * pair + 16, :] = rows


def spatial(order, pieces, weight, down, up):
    vmem = spec(pltpu.VMEM)
    return call(
        spatial_kernel,
        (
            jax.ShapeDtypeStruct((16, 64, 128), BF16),
            jax.ShapeDtypeStruct((8, ROWS, WIDTH), BF16),
            jax.ShapeDtypeStruct((8 * ROWS, 256), F32),
            jax.ShapeDtypeStruct((8 * ROWS, 128), BF16),
            jax.ShapeDtypeStruct((8, ROWS, ROWS), F32),
        ),
        [pltpu.VMEM((WIDTH, 384), BF16), pltpu.SemaphoreType.DMA((8,))],
        [spec(pltpu.SMEM)] + [spec(pl.ANY)] * 8 + [vmem] * 3,
    )(order, *pieces, weight, down, up)


def spatial_back_kernel(cotangent, modded, projected, reduced, weights, up, grad, d_projected):
    for pair in range(4):
        rows = cotangent[:, 16 * pair : 16 * pair + 16, :].astype(F32).reshape(16, 2, 8, 128)
        for side in range(2):
            frame = 2 * pair + side
            span = slice(frame * ROWS, frame * ROWS + ROWS)
            q, k, v = split_heads(projected[span])
            q_out = (q * head_rate(q)).astype(BF16)
            k_out = (k * head_rate(k)).astype(BF16)
            d_q, d_k, d_v = attention_back(
                weights[frame],
                q_out,
                k_out,
                v.astype(BF16),
                rows[:, side].reshape(ROWS, 128).astype(BF16),
            )
            d_projected[span] = join_heads(head_norm_back(q, d_q), head_norm_back(k, d_k), d_v)
    high, rest = halves(d_projected[...])
    both = dot(reduced[...], jnp.concatenate([high, rest], 1), TN)
    grad_up = both[:64, :256] + both[64:, :256] + both[:64, 256:] + both[64:, 256:]
    two = dot(high, up[:128], NT) + dot(rest, up[:128], NT)
    low_high, low_rest = halves(two[:, :64] + two[:, 64:])
    down = dot(
        jnp.concatenate([low_high, low_rest], 1), modded[...].reshape(8 * ROWS, WIDTH), TN
    )
    grad_down = down[:64] + down[64:]
    grad[:64, :640] = grad_down[:, :640]
    grad[:64, 640:] = grad_up[:, :128]
    grad[64:, :512] = grad_down[:, 640:]
    grad[64:, 512:640] = grad_up[:, 128:]
    grad[64:, 640:] = jnp.zeros((64, 128), F32)


def spatial_back(cotangent, modded, projected, reduced, weights, up):
    return call(
        spatial_back_kernel,
        jax.ShapeDtypeStruct((128, 768), F32),
        [pltpu.VMEM((8 * ROWS, 256), F32)],
    )(cotangent, modded, projected, reduced, weights, up)


def assemble_kernel(order, *refs):
    pieces = refs[:8]
    qkv, out_first, out_second, held, sems = refs[8:]
    copies = [
        pltpu.make_async_copy(piece, held.at[order[i]], sems.at[i])
        for i, piece in enumerate(pieces)
    ]
    for copy in copies:
        copy.start()
    for copy in copies:
        copy.wait()

    def step(head, _):
        for d in range(32):
            a, b = 36 * d, 18 * d
            qkv[head, a : a + 36, :128] = held[head, 0, d, 0:36]
            qkv[head, a : a + 18, 128:] = held[head, 0, d, 36:54]
            qkv[head, a + 18 : a + 36, 128:] = held[head, 1, d, 0:18]
        return 0

    lax.fori_loop(0, HEADS, step, 0)
    for head in range(HEADS):
        main = slice(128 * head, 128 * head + 128)
        tail = slice(1024 + 16 * head, 1040 + 16 * head)
        for d in range(32):
            rows = slice(18 * d, 18 * d + 18)
            out_first[rows, main] = held[head, 1, d, 18:36]
            out_second[rows, main] = held[head, 1, d, 36:54]
            out_first[rows, tail] = held[head, 0, d, 36:54, 88:104]
            out_second[rows, tail] = held[head, 1, d, 0:18, 88:104]


def assemble(order, pieces):
    return call(
        assemble_kernel,
        (
            jax.ShapeDtypeStruct((HEADS, WIDTH, 256), BF16),
            jax.ShapeDtypeStruct((FEATURES, WIDTH), BF16),
            jax.ShapeDtypeStruct((FEATURES, WIDTH), BF16),
        ),
        [pltpu.VMEM((8, 2, 32, 54, 128), BF16), pltpu.SemaphoreType.DMA((8,))],
        [spec(pltpu.SMEM)] + [spec(pl.ANY)] * 8,
    )(order, *pieces)


def by_rows(values):
    values = values.astype(F32)
    frames = [x * 4 + l * 2 + c for l in range(2) for x in range(4) for c in range(2)]
    return jnp.concatenate([values[f] for f in frames], 0)


def temporal_kernel(
    received,
    latents,
    targets,
    modulation,
    qkv,
    out_first,
    out_second,
    down,
    up,
    cosine,
    sine,
    sent,
    modded,
    reduced,
    d_projected,
    d_reduced,
    wide,
    projected,
    weights,
    q_all,
    k_all,
    v_all,
):
    for head in range(HEADS):
        x, c = head // 2, head % 2
        rows = jnp.concatenate([received[x * 4 + c], received[x * 4 + 2 + c]], 0).astype(F32)
        wide[:, HEAD * head : HEAD * head + HEAD] = rows[:, :HEAD]
    gate_first, gate_second = modulation[0, 2:3], modulation[1, 2:3]
    mixed = dot(wide[...].astype(BF16), out_first[...])
    middle = (by_rows(latents[...]) + gate_first * mixed).astype(BF16).astype(F32)
    normed, rate = normalise(middle)
    scale = 1.0 + modulation[1, 1:2]
    modded[...] = (normed * scale + modulation[1, 0:1]).astype(BF16)
    low = dot(modded[...], down[...])
    high, rest = halves(low[:, :64] + low[:, 64:])
    reduced[...] = jnp.concatenate([high, rest], 1)
    three = jnp.concatenate([high, high, rest], 1)
    mask = same_token()
    for head in range(HEADS):
        both = dot(modded[...], qkv[head]) + dot(three, up[head])
        projected[head] = both
        q, k, v = split_heads(both)
        q = q * head_rate(q)
        k = k * head_rate(k)
        q = (q * cosine[...] + swap(q) * sine[...]).astype(BF16)
        k = (k * cosine[...] + swap(k) * sine[...]).astype(BF16)
        v = v.astype(BF16)
        w = softmax(dot(q, k, NT), mask)
        q_all[head], k_all[head], v_all[head], weights[head] = q, k, v, w
        wide[:, HEAD * head : HEAD * head + HEAD] = dot(w.astype(BF16), v)[:, :HEAD]
    mixed = dot(wide[...].astype(BF16), out_second[...])
    produced = (middle + gate_second * mixed).astype(BF16).astype(F32)
    error = ((produced - by_rows(targets[...])) / WIDTH).astype(BF16).astype(F32)
    wide[...] = dot((gate_second * error).astype(BF16), out_second[...], NT)
    d_low = jnp.zeros((ROWS, 128), F32)
    d_modded = jnp.zeros((ROWS, WIDTH), F32)
    for head in range(HEADS):
        cotangent = wide[:, HEAD * head : HEAD * head + HEAD].astype(BF16)
        cotangent = jnp.concatenate([cotangent, jnp.zeros((ROWS, 128 - HEAD), BF16)], 1)
        d_q, d_k, d_v = attention_back(
            weights[head], q_all[head], k_all[head], v_all[head], cotangent
        )
        d_q = d_q * cosine[...] - swap(d_q) * sine[...]
        d_k = d_k * cosine[...] - swap(d_k) * sine[...]
        q, k, _ = split_heads(projected[head])
        joined = join_heads(head_norm_back(q, d_q), head_norm_back(k, d_k), d_v)
        d_projected[head] = joined
        high, rest = halves(joined)
        d_low += dot(high, up[head, :128], NT) + dot(rest, up[head, :128], NT)
        d_modded += dot(high, qkv[head], NT)
    d_low = d_low[:, :64] + d_low[:, 64:]
    high, rest = halves(d_low)
    d_reduced[...] = jnp.concatenate([high, rest], 1)
    through = dot(jnp.concatenate([high, high], 1), down[...], NT) + dot(
        rest, down[:, :64], NT
    )
    d_modded = (d_modded.astype(BF16) + through.astype(BF16)).astype(F32)
    d_normed = d_modded * scale
    inner = jnp.mean(d_normed * normed, -1, keepdims=True)
    d_middle = rate * (d_normed - jnp.mean(d_normed, -1, keepdims=True) - normed * inner)
    d_middle = (error.astype(BF16) + d_middle.astype(BF16)).astype(F32)
    wide[...] = dot((gate_first * d_middle).astype(BF16), out_first[...], NT)
    for head in range(HEADS):
        x, c = head // 2, head % 2
        rows = wide[:, HEAD * head : HEAD * head + HEAD].astype(BF16)
        rows = jnp.concatenate([rows, jnp.zeros((ROWS, 128 - HEAD), BF16)], 1)
        sent[x * 4 + c] = rows[:64]
        sent[x * 4 + 2 + c] = rows[64:]


def temporal(*operands):
    return call(
        temporal_kernel,
        (
            jax.ShapeDtypeStruct((16, 64, 128), BF16),
            jax.ShapeDtypeStruct((ROWS, WIDTH), BF16),
            jax.ShapeDtypeStruct((ROWS, 128), BF16),
            jax.ShapeDtypeStruct((HEADS, ROWS, 256), F32),
            jax.ShapeDtypeStruct((ROWS, 128), BF16),
        ),
        [
            pltpu.VMEM((ROWS, FEATURES), F32),
            pltpu.VMEM((HEADS, ROWS, 256), F32),
            pltpu.VMEM((HEADS, ROWS, ROWS), F32),
            pltpu.VMEM((HEADS, ROWS, 128), BF16),
            pltpu.VMEM((HEADS, ROWS, 128), BF16),
            pltpu.VMEM((HEADS, ROWS, 128), BF16),
        ],
    )(*operands)


def temporal_grad_kernel(modded, reduced, d_projected, d_reduced, grad, ups):
    for head in range(HEADS):
        high, rest = halves(d_projected[head])
        both = dot(reduced[...], jnp.concatenate([high, rest], 1), TN)
        part = both[:64, :256] + both[64:, :256] + both[:64, 256:] + both[64:, 256:]
        for k in range(3):
            start = k * FEATURES + head * HEAD
            ups[:, start : start + HEAD] = part[:, k * HEAD : k * HEAD + HEAD]
    down = dot(d_reduced[...], modded[...], TN)
    grad[:64, :WIDTH] = down[:64] + down[64:]
    grad[:64, WIDTH:] = ups[:, :384]
    grad[64:, :1280] = ups[:, 384:1664]
    grad[64:, 1280:1408] = jnp.concatenate([ups[:, 1664:], jnp.zeros((64, 64), F32)], 1)
    grad[64:, 1408:] = jnp.zeros((64, 128), F32)


def temporal_grad(*operands):
    return call(
        temporal_grad_kernel,
        jax.ShapeDtypeStruct((128, 1536), F32),
        [pltpu.VMEM((64, 3 * FEATURES), F32)],
    )(*operands)


def epilogue_kernel(spatial_sum, temporal_sum, grad_down, grad_up):
    first = spatial_sum[...].reshape(128, 1664)
    second = temporal_sum[...].reshape(128, 1536)
    down = jnp.concatenate([first[:64, :640], first[64:, :512]], 1)
    grad_down[0] = down.T
    grad_down[1] = second[:64, :WIDTH].T
    for head in range(HEADS):
        top = first[:64, 640 + 128 * head : 768 + 128 * head]
        bottom = first[64:, 640 + 128 * head : 768 + 128 * head]
        both = jnp.concatenate([top, bottom], 1)
        for k in range(3):
            start = k * FEATURES + head * HEAD
            grad_up[0, :, start : start + HEAD] = both[:, k * HEAD : k * HEAD + HEAD]
    grad_up[1, :, :384] = second[:64, WIDTH:]
    grad_up[1, :, 384:] = second[64:, :1344]


def epilogue(spatial_sum, temporal_sum):
    return call(
        epilogue_kernel,
        (
            jax.ShapeDtypeStruct((2, WIDTH, RANK), F32),
            jax.ShapeDtypeStruct((2, RANK, 3 * FEATURES), F32),
        ),
    )(spatial_sum, temporal_sum)


def exchange(values, axes):
    return lax.all_to_all(values, axes, 0, 0)


def spread(values, axes, count):
    return exchange(jnp.broadcast_to(values[None], (count,) + values.shape), axes)


def shift(values, axis, count, by):
    return lax.ppermute(values, axis, [(i, (i + by) % count) for i in range(count)])


def two_parts(values):
    high = lax.reduce_precision(values, 8, 7)
    return high.astype(BF16), (values - high).astype(BF16)


def on_device(latents, targets, modulation, qkv, out, down, up):
    x, l, c = lax.axis_index("x"), lax.axis_index("l"), lax.axis_index("c")
    place = jnp.stack([x * 2 + c, l]).astype(jnp.int32)
    order = jnp.stack(
        [((x - dx) % 4) * 2 + (c ^ dc) for dc in range(2) for dx in range(4)]
    ).astype(jnp.int32)
    modulation = modulation[0]
    modded, first_part, rest_part = prologue(place, latents[0, 0], modulation, qkv, out)

    def around(values):
        along = [values] + [shift(values, "x", 4, by) for by in (1, 2, 3)]
        return along + [shift(v, "c", 2, 1) for v in along]

    pieces = around(modded)
    rest = exchange(rest_part, DP)
    first = exchange(first_part, DP)

    down_high, down_low = two_parts(down)
    down_parts = jnp.concatenate([down_high, down_low], 2)
    by_head = up.reshape(2, RANK, 3, HEADS, HEAD).transpose(0, 3, 1, 2, 4)
    by_head = jnp.pad(by_head.reshape(2, HEADS, RANK, 3 * HEAD), ((0, 0), (0, 0), (0, 0), (0, 40)))
    up_high, up_low = two_parts(by_head)
    up_parts = jnp.concatenate([up_high, up_low, up_high], 2)
    up_mine = lax.dynamic_index_in_dim(up_parts[0], place[0], 0, keepdims=False)

    other = shift(rest, "l", 2, 1)
    rest = jnp.stack([jnp.where(l == 0, rest, other), jnp.where(l == 0, other, rest)])
    qkv_second, out_first, out_second = assemble(order, around(rest))

    both = jnp.stack([latents[0, 0].reshape(16, 8, WIDTH), targets[0, 0].reshape(16, 8, WIDTH)], 1)
    both = exchange(both, SEQ)

    attended, modded_all, projected, reduced, weights = spatial(
        order, pieces, first, down_parts[0], up_mine
    )
    received = exchange(attended, SEQ)
    cosine, sine = rotation_tables()
    sent, modded_rows, low, d_projected, d_low = temporal(
        received,
        both[:, 0],
        both[:, 1],
        modulation,
        qkv_second,
        out_first,
        out_second,
        down_parts[1],
        up_parts[1],
        jnp.asarray(cosine),
        jnp.asarray(sine),
    )
    cotangent = exchange(sent, SEQ)
    late = temporal_grad(modded_rows, low, d_projected, d_low).reshape(16, 8, 1536)
    late = jnp.sum(exchange(late, SEQ), 0)
    early = spatial_back(cotangent, modded_all, projected, reduced, weights, up_mine)
    early = exchange(early.reshape(16, 8, 768), SEQ)
    early_down = jnp.sum(early[:, :, :640], 0)
    early_up = jnp.sum(early[:, :, 640:].reshape(4, 2, 2, 8, 128), 1)
    early_up = early_up.reshape(8, 8, 128).transpose(1, 0, 2).reshape(8, 1024)
    bottom_up = jnp.sum(early[:, :, 512:640].reshape(4, 2, 2, 8, 128), 1)
    bottom_up = bottom_up.reshape(8, 8, 128).transpose(1, 0, 2).reshape(8, 1024)
    bottom = place[0] * 0 + (x >= 2).astype(jnp.int32)
    early_up = jnp.where(bottom == 1, bottom_up, early_up)
    total = jnp.concatenate([early_down, early_up, late], 1)
    total = jnp.sum(spread(total, ("z",), 8), 0)
    total = jnp.sum(spread(total, ("h",), 4), 0)
    total = spread(total, SEQ, 16)
    return epilogue(total[:, :, :1664], total[:, :, 1664:])


def solution(mesh):
    inner = Mesh(mesh.devices.reshape(8, 4, 4, 2, 2), ("z", "h", "x", "l", "c"))
    in_specs = (
        P(DP, SEQ, None, None),
        P(DP, SEQ, None, None),
        P(DP, None, None, None),
        P(None, DP, None),
        P(None, DP, None),
        P(),
        P(),
    )
    return jax.shard_map(
        on_device, mesh=inner, in_specs=in_specs, out_specs=(P(), P()), check_vma=False
    )
```

```python
import math

import jax
import jax.numpy as jnp
import numpy as np
from jax import lax
from jax.experimental import pallas as pl
from jax.experimental.pallas import tpu as pltpu
from jax.sharding import Mesh, PartitionSpec as P

WIDTH = 1152
HEADS = 8
HEAD = 72
RANK = 64
FEATURES = HEADS * HEAD
ROWS = 128
F32 = jnp.float32
BF16 = jnp.bfloat16
SCALE = 1.0 / math.sqrt(HEAD)
MIB = 1 << 20
DP = ("z", "h")
SEQ = ("x", "l", "c")


def call(kernel, out_shape, scratch=(), in_specs=None, limit=16):
    vmem = pl.BlockSpec(memory_space=pltpu.VMEM)

    def run(*operands):
        return pl.pallas_call(
            kernel,
            out_shape=out_shape,
            in_specs=in_specs or [vmem] * len(operands),
            out_specs=jax.tree.map(lambda _: vmem, out_shape),
            scratch_shapes=list(scratch),
            compiler_params=pltpu.CompilerParams(vmem_limit_bytes=limit * MIB),
        )(*operands)

    return run


def spec(space):
    return pl.BlockSpec(memory_space=space)


def dot(a, b, dims=((1,), (0,))):
    return lax.dot_general(a, b, (dims, ((), ())), preferred_element_type=F32)


NT = ((1,), (1,))
TN = ((0,), (0,))


def halves(values):
    high = values.astype(BF16)
    return high, (values - high.astype(F32)).astype(BF16)


def normalise(values):
    centred = values - jnp.mean(values, -1, keepdims=True)
    rate = lax.rsqrt(jnp.mean(centred * centred, -1, keepdims=True) + 1e-06)
    return centred * rate, rate


def lane_mask(width, dtype=F32):
    lanes = lax.broadcasted_iota(jnp.int32, (1, 128), 1)
    return (lanes < width).astype(dtype)


def split_heads(projected):
    keep = lane_mask(HEAD)
    q = projected[:, :128] * keep
    k = pltpu.roll(projected, 256 - HEAD, 1)[:, :128] * keep
    v = pltpu.roll(projected, 256 - 2 * HEAD, 1)[:, :128] * keep
    return q, k, v


def join_heads(q, k, v):
    zero = jnp.zeros_like(q)
    return (
        jnp.concatenate([q, zero], 1)
        + pltpu.roll(jnp.concatenate([k, zero], 1), HEAD, 1)
        + pltpu.roll(jnp.concatenate([v, zero], 1), 2 * HEAD, 1)
    )


def head_rate(values):
    return lax.rsqrt(jnp.sum(values * values, -1, keepdims=True) * (1.0 / HEAD) + 1e-06)


def head_norm_back(values, cotangent):
    rate = head_rate(values)
    inner = jnp.sum(cotangent * values, -1, keepdims=True) * (1.0 / HEAD)
    return rate * (cotangent - values * (rate * rate * inner))


def swap(values):
    lanes = lax.broadcasted_iota(jnp.int32, (1, 128), 1)
    return jnp.where(
        lanes < HEAD // 2,
        pltpu.roll(values, 128 - HEAD // 2, 1),
        pltpu.roll(values, HEAD // 2, 1),
    )


def softmax(scores, mask):
    weights = jnp.exp(scores * SCALE)
    if mask is not None:
        weights = weights * mask
    return weights / jnp.sum(weights, -1, keepdims=True)


def attention_back(weights, q, k, v, cotangent):
    rounded = weights.astype(BF16)
    d_v = dot(rounded, cotangent, TN).astype(BF16)
    d_weights = dot(cotangent, v, NT).astype(BF16).astype(F32)
    d_scores = weights * (d_weights - jnp.sum(d_weights * weights, -1, keepdims=True))
    d_scores = (d_scores * SCALE).astype(BF16)
    d_q = dot(d_scores, k).astype(BF16)
    d_k = dot(d_scores, q, TN).astype(BF16)
    return d_q.astype(F32), d_k.astype(F32), d_v.astype(F32)


def same_token():
    rows = lax.broadcasted_iota(jnp.int32, (ROWS, ROWS), 0)
    columns = lax.broadcasted_iota(jnp.int32, (ROWS, ROWS), 1)
    return ((rows & 7) == (columns & 7)).astype(F32)


def rotation_tables():
    row = np.arange(ROWS)
    frame = ((row // 16) % 4) * 4 + (row // 64) * 2 + (row // 8) % 2
    half = HEAD // 2
    frequency = np.exp(np.arange(half) * (-2.0 * math.log(10000.0) / HEAD))
    angle = frame[:, None] * frequency[None, :]
    cosine = np.zeros((ROWS, 128), np.float32)
    sine = np.zeros((ROWS, 128), np.float32)
    cosine[:, :half] = cosine[:, half:HEAD] = np.cos(angle)
    sine[:, :half] = -np.sin(angle)
    sine[:, half:HEAD] = np.sin(angle)
    return cosine, sine


def prologue_kernel(place, *refs):
    sources, (modded, part, first_part), held = refs[:4], refs[4:7], refs[7:11]
    rest, sems = refs[11:]
    copies = [pltpu.make_async_copy(a, b, sems.at[i]) for i, (a, b) in enumerate(zip(sources, held))]
    for copy in copies:
        copy.start()
    latents, modulation, qkv, out = held
    rest[...] = jnp.zeros_like(rest)
    copies[0].wait()
    copies[1].wait()
    normed, _ = normalise(latents[...].astype(F32))
    modded[...] = (normed * (1.0 + modulation[0, 1:2]) + modulation[0, 0:1]).astype(BF16)
    copies[2].wait()
    copies[3].wait()
    for head in range(HEADS):

        @pl.when(place[0] == head)
        def _():
            for k in range(3):
                columns = slice(k * FEATURES + head * HEAD, k * FEATURES + head * HEAD + HEAD)
                rest[0, :, k * HEAD : k * HEAD + HEAD] = qkv[0, :, columns].astype(F32)
                rest[1, :, k * HEAD : k * HEAD + HEAD] = qkv[1, :, columns].astype(F32)
            for block in range(2):
                rows = slice(18 * block, 18 * block + 18)
                rest[1, rows, 216:232] = out[block, :, 1024 + 16 * head : 1040 + 16 * head].astype(F32)
                rest[1, rows, 256:384] = out[block, :, 128 * head : 128 * head + 128].astype(F32)

    lower = place[1] == 0
    first = rest[0, :, :256].astype(BF16)
    tiles = jnp.concatenate([rest[1, :, 128 * t : 128 * t + 128] for t in range(3)], 0)
    mine = jnp.where(lower, tiles[:54], tiles[54:])
    mine = jnp.concatenate([mine, jnp.zeros((2, 128), F32)], 0).astype(BF16)
    for copy in range(32):
        part[copy] = mine
        first_part[copy, :36] = first


def prologue(place, *operands):
    return call(
        prologue_kernel,
        (
            jax.ShapeDtypeStruct((ROWS, WIDTH), BF16),
            jax.ShapeDtypeStruct((32, 56, 128), BF16),
            jax.ShapeDtypeStruct((32, 40, 256), BF16),
        ),
        [pltpu.VMEM(v.shape, v.dtype) for v in operands]
        + [pltpu.VMEM((2, 36, 384), F32), pltpu.SemaphoreType.DMA((4,))],
        [spec(pltpu.SMEM)] + [spec(pl.ANY)] * 4,
    )(place, *operands)


def adapters_kernel(down, up, down_parts, up_parts):
    for block in range(2):
        high, low = halves(down[block])
        down_parts[block, :64] = high
        down_parts[block, 64:] = low
        for head in range(HEADS):
            start = head * HEAD
            columns = [up[block, :, k * FEATURES + start : k * FEATURES + start + HEAD] for k in range(3)]
            zero = jnp.zeros((RANK, 128 - HEAD), F32)
            wide = join_heads(*[jnp.concatenate([part, zero], 1) for part in columns])
            high, low = halves(wide)
            up_parts[block, head, :64] = high
            up_parts[block, head, 64:128] = low
            up_parts[block, head, 128:] = high


def adapters(down, up):
    return call(
        adapters_kernel,
        (
            jax.ShapeDtypeStruct((2, 128, WIDTH), BF16),
            jax.ShapeDtypeStruct((2, HEADS, 192, 256), BF16),
        ),
    )(down, up)


def spatial_kernel(
    place,
    modded,
    weight,
    down,
    up,
    latents,
    targets,
    sent,
    projected,
    reduced,
    weights,
    merged,
):
    for chunk in range(32):
        merged[36 * chunk : 36 * chunk + 36, :] = weight[chunk, :36]
    sent[:, :, 1024 : 1024 + WIDTH] = latents[...].astype(F32).reshape(16, 8, WIDTH).astype(BF16)
    sent[:, :, 1024 + WIDTH :] = targets[...].astype(F32).reshape(16, 8, WIDTH).astype(BF16)
    rows = modded[...].reshape(8 * ROWS, WIDTH)
    low = dot(rows, down[0], NT)
    high, rest = halves(low[:, :64] + low[:, 64:])
    reduced[...] = jnp.concatenate([high, rest], 1)
    adapted = dot(jnp.concatenate([high, high, rest], 1), up[0, place[0]])
    projected[...] = dot(rows, merged[...]) + adapted
    for frame in range(8):
        q, k, v = split_heads(projected[frame * ROWS : frame * ROWS + ROWS])
        q = (q * head_rate(q)).astype(BF16)
        k = (k * head_rate(k)).astype(BF16)
        w = softmax(dot(q, k, NT), None)
        weights[frame] = w
        attended = dot(w.astype(BF16), v.astype(BF16)).reshape(16, 8, 128)
        sent[:, :, 128 * frame : 128 * frame + 128] = attended.astype(BF16)


def spatial(place, *operands):
    return call(
        spatial_kernel,
        (
            jax.ShapeDtypeStruct((16, 8, 1024 + 2 * WIDTH), BF16),
            jax.ShapeDtypeStruct((8 * ROWS, 256), F32),
            jax.ShapeDtypeStruct((8 * ROWS, 128), BF16),
            jax.ShapeDtypeStruct((8, ROWS, ROWS), F32),
        ),
        [pltpu.VMEM((WIDTH, 256), BF16)],
        [spec(pltpu.SMEM)] + [spec(pltpu.VMEM)] * 6,
        limit=24,
    )(place, *operands)


def spatial_back_kernel(place, cotangent, modded, projected, reduced, weights, up, grad, d_projected):
    for pair in range(4):
        rows = cotangent[:, 16 * pair : 16 * pair + 16, :].astype(F32).reshape(16, 2, 8, 128)
        for side in range(2):
            frame = 2 * pair + side
            span = slice(frame * ROWS, frame * ROWS + ROWS)
            q, k, v = split_heads(projected[span])
            q_out = (q * head_rate(q)).astype(BF16)
            k_out = (k * head_rate(k)).astype(BF16)
            d_q, d_k, d_v = attention_back(
                weights[frame],
                q_out,
                k_out,
                v.astype(BF16),
                rows[:, side].reshape(ROWS, 128).astype(BF16),
            )
            d_projected[span] = join_heads(head_norm_back(q, d_q), head_norm_back(k, d_k), d_v)
    high, rest = halves(d_projected[...])
    both = dot(reduced[...], jnp.concatenate([high, rest], 1), TN)
    grad_up = both[:64, :256] + both[64:, :256] + both[:64, 256:] + both[64:, 256:]
    head = up[0, place[0], :128]
    two = dot(high, head, NT) + dot(rest, head, NT)
    low_high, low_rest = halves(two[:, :64] + two[:, 64:])
    down = dot(
        jnp.concatenate([low_high, low_rest], 1), modded[...].reshape(8 * ROWS, WIDTH), TN
    )
    store_tiles(grad, 0, down[:64] + down[64:])
    store_tiles(grad, 9, grad_up)


def store_tiles(ref, start, values):
    for tile in range(values.shape[1] // 128):
        ref[:, start + tile, :] = values[:, 128 * tile : 128 * tile + 128]


def spatial_back(*operands):
    vmem = spec(pltpu.VMEM)
    return call(
        spatial_back_kernel,
        jax.ShapeDtypeStruct((RANK, 11, 128), F32),
        [pltpu.VMEM((8 * ROWS, 256), F32)],
        [spec(pltpu.SMEM)] + [vmem] * 6,
        limit=24,
    )(*operands)


def assemble(parts, held, sems, qkv, out_first, out_second):
    for x in range(4):
        copy = part_copy(parts, held, sems, x)
        copy.wait()
        for c in range(2):
            head = 2 * x + c
            lower, upper = held.at[4 * x + c], held.at[4 * x + 2 + c]
            main = slice(128 * head, 128 * head + 128)
            tail = slice(1024 + 16 * head, 1040 + 16 * head)
            for d in range(32):
                a = 36 * d
                qkv[head, a : a + 36, :128] = lower[d, 0:36]
                qkv[head, a : a + 18, 128:] = lower[d, 36:54]
                qkv[head, a + 18 : a + 36, 128:] = upper[d, 0:18]
                rows = slice(18 * d, 18 * d + 18)
                out_first[rows, main] = upper[d, 18:36]
                out_second[rows, main] = upper[d, 36:54]
                out_first[rows, tail] = lower[d, 36:54, 88:104]
                out_second[rows, tail] = upper[d, 0:18, 88:104]


def part_copy(parts, held, sems, x):
    span = pl.ds(4 * x, 4)
    return pltpu.make_async_copy(parts.at[span], held.at[span], sems.at[x])


def by_rows(received, columns):
    values = received[:, :, columns].astype(F32)
    frames = [x * 4 + l * 2 + c for l in range(2) for x in range(4) for c in range(2)]
    return jnp.concatenate([values[f] for f in frames], 0)


def temporal_kernel(
    received,
    modulation,
    parts,
    down,
    up,
    cosine,
    sine,
    sent,
    grad,
    wide,
    modded,
    reduced,
    d_projected,
    ups,
    projected,
    weights,
    q_all,
    k_all,
    v_all,
    held,
    qkv,
    out_first,
    out_second,
    sems,
):
    for x in range(4):
        part_copy(parts, held, sems, x).start()
    for head in range(HEADS):
        x, c = head // 2, head % 2
        rows = jnp.concatenate(
            [
                received[x * 4 + 2 * l + c, :, 128 * g : 128 * g + 128].astype(F32)
                for l in range(2)
                for g in range(8)
            ],
            0,
        )
        wide[:, HEAD * head : HEAD * head + HEAD] = rows[:, :HEAD]
    assemble(parts, held, sems, qkv, out_first, out_second)
    gate_first, gate_second = modulation[0, 2:3], modulation[1, 2:3]
    mixed = dot(wide[...].astype(BF16), out_first[...])
    middle = (by_rows(received, slice(1024, 1024 + WIDTH)) + gate_first * mixed).astype(BF16).astype(F32)
    normed, rate = normalise(middle)
    scale = 1.0 + modulation[1, 1:2]
    modded[...] = (normed * scale + modulation[1, 0:1]).astype(BF16)
    low = dot(modded[...], down[1], NT)
    high, rest = halves(low[:, :64] + low[:, 64:])
    reduced[...] = jnp.concatenate([high, rest], 1)
    three = jnp.concatenate([high, high, rest], 1)
    mask = same_token()
    for head in range(HEADS):
        both = dot(modded[...], qkv[head]) + dot(three, up[1, head])
        projected[head] = both
        q, k, v = split_heads(both)
        q = q * head_rate(q)
        k = k * head_rate(k)
        q = (q * cosine[...] + swap(q) * sine[...]).astype(BF16)
        k = (k * cosine[...] + swap(k) * sine[...]).astype(BF16)
        v = v.astype(BF16)
        w = softmax(dot(q, k, NT), mask)
        q_all[head], k_all[head], v_all[head], weights[head] = q, k, v, w
        wide[:, HEAD * head : HEAD * head + HEAD] = dot(w.astype(BF16), v)[:, :HEAD]
    mixed = dot(wide[...].astype(BF16), out_second[...])
    produced = (middle + gate_second * mixed).astype(BF16).astype(F32)
    error = ((produced - by_rows(received, slice(1024 + WIDTH, None))) / WIDTH).astype(BF16).astype(F32)
    wide[...] = dot((gate_second * error).astype(BF16), out_second[...], NT)
    d_low = jnp.zeros((ROWS, 128), F32)
    d_modded = jnp.zeros((ROWS, WIDTH), F32)
    for head in range(HEADS):
        cotangent = wide[:, HEAD * head : HEAD * head + HEAD].astype(BF16)
        cotangent = jnp.concatenate([cotangent, jnp.zeros((ROWS, 128 - HEAD), BF16)], 1)
        d_q, d_k, d_v = attention_back(
            weights[head], q_all[head], k_all[head], v_all[head], cotangent
        )
        d_q = d_q * cosine[...] - swap(d_q) * sine[...]
        d_k = d_k * cosine[...] - swap(d_k) * sine[...]
        q, k, _ = split_heads(projected[head])
        joined = join_heads(head_norm_back(q, d_q), head_norm_back(k, d_k), d_v)
        d_projected[head] = joined
        high, rest = halves(joined)
        d_low += dot(high, up[1, head, :128], NT) + dot(rest, up[1, head, :128], NT)
        d_modded += dot(high, qkv[head], NT)
    d_low = d_low[:, :64] + d_low[:, 64:]
    high, rest = halves(d_low)
    d_reduced = jnp.concatenate([high, rest], 1)
    through = dot(jnp.concatenate([high, high], 1), down[1]) + dot(rest, down[1, :64])
    d_modded = (d_modded.astype(BF16) + through.astype(BF16)).astype(F32)
    d_normed = d_modded * scale
    inner = jnp.mean(d_normed * normed, -1, keepdims=True)
    d_middle = rate * (d_normed - jnp.mean(d_normed, -1, keepdims=True) - normed * inner)
    d_middle = (error.astype(BF16) + d_middle.astype(BF16)).astype(F32)
    wide[...] = dot((gate_first * d_middle).astype(BF16), out_first[...], NT)
    for head in range(HEADS):
        x, c = head // 2, head % 2
        rows = wide[:, HEAD * head : HEAD * head + HEAD].astype(BF16)
        rows = jnp.concatenate([rows, jnp.zeros((ROWS, 128 - HEAD), BF16)], 1)
        sent[x * 4 + c] = rows[:64]
        sent[x * 4 + 2 + c] = rows[64:]
    ups[:, 1664:] = jnp.zeros((64, 128), F32)
    for head in range(HEADS):
        high, rest = halves(d_projected[head])
        both = dot(reduced[...], jnp.concatenate([high, rest], 1), TN)
        part = both[:64, :256] + both[64:, :256] + both[:64, 256:] + both[64:, 256:]
        for k in range(3):
            start = k * FEATURES + head * HEAD
            ups[:, start : start + HEAD] = part[:, k * HEAD : k * HEAD + HEAD]
    down = dot(d_reduced, modded[...], TN)
    store_tiles(grad, 0, down[:64] + down[64:])
    store_tiles(grad, 9, ups[...])


def temporal(*operands):
    return call(
        temporal_kernel,
        (
            jax.ShapeDtypeStruct((16, 64, 128), BF16),
            jax.ShapeDtypeStruct((RANK, 23, 128), F32),
        ),
        [
            pltpu.VMEM((ROWS, FEATURES), F32),
            pltpu.VMEM((ROWS, WIDTH), BF16),
            pltpu.VMEM((ROWS, 128), BF16),
            pltpu.VMEM((HEADS, ROWS, 256), F32),
            pltpu.VMEM((RANK, 1792), F32),
            pltpu.VMEM((HEADS, ROWS, 256), F32),
            pltpu.VMEM((HEADS, ROWS, ROWS), F32),
            pltpu.VMEM((HEADS, ROWS, 128), BF16),
            pltpu.VMEM((HEADS, ROWS, 128), BF16),
            pltpu.VMEM((HEADS, ROWS, 128), BF16),
            pltpu.VMEM((16, 32, 56, 128), BF16),
            pltpu.VMEM((HEADS, WIDTH, 256), BF16),
            pltpu.VMEM((FEATURES, WIDTH), BF16),
            pltpu.VMEM((FEATURES, WIDTH), BF16),
            pltpu.SemaphoreType.DMA((4,)),
        ],
        [spec(pltpu.VMEM)] * 2 + [spec(pl.ANY)] + [spec(pltpu.VMEM)] * 4,
        limit=32,
    )(*operands)


def epilogue_kernel(place, own, other, grad_down, grad_up):
    for side, ref in enumerate((own, other)):
        core = place[2] if side == 0 else 1 - place[2]
        rows = pl.ds(pl.multiple_of(core * 32, 32), 32)
        for tile in range(9):
            columns = slice(128 * tile, 128 * tile + 128)
            grad_down[0, rows, columns] = ref[:, tile, :]
            grad_down[1, rows, columns] = ref[:, 25 + tile, :]
        for head in range(HEADS):
            both = jnp.concatenate([ref[:, 9 + 2 * head, :], ref[:, 10 + 2 * head, :]], 1)
            for k in range(3):
                start = k * FEATURES + head * HEAD
                grad_up[0, rows, start : start + HEAD] = both[:, k * HEAD : k * HEAD + HEAD]
        for tile in range(13):
            grad_up[1, rows, 128 * tile : 128 * tile + 128] = ref[:, 34 + tile, :]
        grad_up[1, rows, 1664:1728] = ref[:, 47, :][:, :64]


def epilogue(place, own, other):
    vmem = spec(pltpu.VMEM)
    return call(
        epilogue_kernel,
        (
            jax.ShapeDtypeStruct((2, RANK, WIDTH), F32),
            jax.ShapeDtypeStruct((2, RANK, 3 * FEATURES), F32),
        ),
        in_specs=[spec(pltpu.SMEM), vmem, vmem],
    )(place, own, other)


def exchange(values, axes):
    return lax.all_to_all(values, axes, 0, 0)


def spread(values, axes, count):
    return exchange(jnp.broadcast_to(values[None], (count,) + values.shape), axes)


def swap_cores(values):
    return lax.ppermute(values, "c", [(0, 1), (1, 0)])


def add_cores(values, c):
    mine = lax.dynamic_slice_in_dim(values, c * 32, 32, 0)
    return mine, swap_cores(lax.dynamic_slice_in_dim(values, (1 - c) * 32, 32, 0))


def on_device(latents, targets, modulation, qkv, out, down, up):
    x, l, c = lax.axis_index("x"), lax.axis_index("l"), lax.axis_index("c")
    place = jnp.stack([x * 2 + c, l, c]).astype(jnp.int32)
    modulation = modulation[0]
    modded, part, first = prologue(place, latents[0, 0], modulation, qkv, out)
    modded = lax.all_gather(modded, ("x", "c"), axis=0, tiled=False)
    parts = lax.all_gather(exchange(part, DP), SEQ, axis=0, tiled=False)
    first = exchange(first, DP)
    down_parts, up_parts = adapters(down.transpose(0, 2, 1), up)
    sent, projected, reduced, weights = spatial(
        place, modded, first, down_parts, up_parts, latents[0, 0], targets[0, 0]
    )
    received = exchange(sent, SEQ)
    cosine, sine = rotation_tables()
    sent, late = temporal(
        received,
        modulation,
        parts,
        down_parts,
        up_parts,
        jnp.asarray(cosine),
        jnp.asarray(sine),
    )
    cotangent = exchange(sent, SEQ)
    late = sum(add_cores(late, c))
    early = spatial_back(place, cotangent, modded, projected, reduced, weights, up_parts)
    mine, other = add_cores(early, c)
    first_up, second_up = mine[:, 9:], other[:, 9:]
    total = jnp.concatenate(
        [
            mine[:, :9] + other[:, :9],
            jnp.where(c == 0, first_up, second_up),
            jnp.where(c == 0, second_up, first_up),
            late,
        ],
        1,
    )
    total = exchange(total.reshape(32, 9, 4, 128), ("z", "x")).reshape(32, 36, 128)
    ups = jnp.sum(total[:, 9:13].reshape(8, 4, 4, 128), 0).reshape(16, 128)
    total = jnp.concatenate([jnp.sum(total[:, :9], 0), ups, jnp.sum(total[:, 13:], 0)], 0)
    total = jnp.sum(spread(total, ("h", "l"), 8), 0)
    total = spread(total, ("z", "x"), 32)
    grad_down, grad_up = epilogue(place, total, swap_cores(total))
    return grad_down.transpose(0, 2, 1), grad_up


def solution(mesh):
    inner = Mesh(mesh.devices.reshape(8, 4, 4, 2, 2), ("z", "h", "x", "l", "c"))
    in_specs = (
        P(DP, SEQ, None, None),
        P(DP, SEQ, None, None),
        P(DP, None, None, None),
        P(None, DP, None),
        P(None, DP, None),
        P(),
        P(),
    )
    return jax.shard_map(
        on_device, mesh=inner, in_specs=in_specs, out_specs=(P(), P()), check_vma=False
    )
```

```python
import math

import jax
import jax.numpy as jnp
import numpy as np
from jax import lax
from jax.experimental import pallas as pl
from jax.experimental.pallas import tpu as pltpu
from jax.sharding import Mesh, PartitionSpec as P

WIDTH = 1152
HEADS = 8
HEAD = 72
RANK = 64
FEATURES = HEADS * HEAD
ROWS = 128
F32 = jnp.float32
BF16 = jnp.bfloat16
SCALE = 1.0 / math.sqrt(HEAD)
MIB = 1 << 20
DP = ("z", "h")
SEQ = ("x", "l", "c")


def call(kernel, out_shape, scratch=(), in_specs=None, limit=20, out_space=pltpu.VMEM, us=2):
    vmem = pl.BlockSpec(memory_space=pltpu.VMEM)
    out_spec = pl.BlockSpec(memory_space=out_space)

    def run(*operands):
        return pl.pallas_call(
            kernel,
            out_shape=out_shape,
            in_specs=in_specs or [vmem] * len(operands),
            out_specs=jax.tree.map(lambda _: out_spec, out_shape),
            scratch_shapes=list(scratch),
            compiler_params=pltpu.CompilerParams(vmem_limit_bytes=limit * MIB),
            cost_estimate=pl.CostEstimate(
                flops=us * 10**9, bytes_accessed=us * 3 * 10**6, transcendentals=0
            ),
        )(*operands)

    return run


def spec(space):
    return pl.BlockSpec(memory_space=space)


SMEM, VMEM, HBM = spec(pltpu.SMEM), spec(pltpu.VMEM), spec(pltpu.HBM)


def copier(sems):
    count = iter(range(100))

    def start(source, target):
        copy = pltpu.make_async_copy(source, target, sems.at[next(count)])
        copy.start()
        return copy

    return start


def like(values):
    return pltpu.VMEM(values.shape, values.dtype)


def dot(a, b, dims=((1,), (0,))):
    return lax.dot_general(a, b, (dims, ((), ())), preferred_element_type=F32)


NT = ((1,), (1,))
TN = ((0,), (0,))


def halves(values):
    high = values.astype(BF16)
    return high, (values - high.astype(F32)).astype(BF16)


def normalise(values):
    centred = values - jnp.mean(values, -1, keepdims=True)
    rate = lax.rsqrt(jnp.mean(centred * centred, -1, keepdims=True) + 1e-06)
    return centred * rate, rate


def lane_mask(width, dtype=F32):
    lanes = lax.broadcasted_iota(jnp.int32, (1, 128), 1)
    return (lanes < width).astype(dtype)


def split_heads(projected):
    keep = lane_mask(HEAD)
    q = projected[:, :128] * keep
    k = pltpu.roll(projected, 256 - HEAD, 1)[:, :128] * keep
    v = pltpu.roll(projected, 256 - 2 * HEAD, 1)[:, :128] * keep
    return q, k, v


def join_heads(q, k, v):
    zero = jnp.zeros_like(q)
    return (
        jnp.concatenate([q, zero], 1)
        + pltpu.roll(jnp.concatenate([k, zero], 1), HEAD, 1)
        + pltpu.roll(jnp.concatenate([v, zero], 1), 2 * HEAD, 1)
    )


def head_rate(values):
    return lax.rsqrt(jnp.sum(values * values, -1, keepdims=True) * (1.0 / HEAD) + 1e-06)


def head_norm_back(values, cotangent):
    rate = head_rate(values)
    inner = jnp.sum(cotangent * values, -1, keepdims=True) * (1.0 / HEAD)
    return rate * (cotangent - values * (rate * rate * inner))


def swap(values):
    lanes = lax.broadcasted_iota(jnp.int32, (1, 128), 1)
    return jnp.where(
        lanes < HEAD // 2,
        pltpu.roll(values, 128 - HEAD // 2, values.ndim - 1),
        pltpu.roll(values, HEAD // 2, values.ndim - 1),
    )


def softmax(scores, mask):
    weights = jnp.exp(scores * SCALE)
    if mask is not None:
        weights = weights * mask
    return weights / jnp.sum(weights, -1, keepdims=True)


def attention_back(weights, q, k, v, cotangent):
    rounded = weights.astype(BF16)
    d_v = dot(rounded, cotangent, TN).astype(BF16)
    d_weights = dot(cotangent, v, NT).astype(BF16).astype(F32)
    d_scores = weights * (d_weights - jnp.sum(d_weights * weights, -1, keepdims=True))
    d_scores = (d_scores * SCALE).astype(BF16)
    d_q = dot(d_scores, k).astype(BF16)
    d_k = dot(d_scores, q, TN).astype(BF16)
    return d_q.astype(F32), d_k.astype(F32), d_v.astype(F32)


def same_token():
    rows = lax.broadcasted_iota(jnp.int32, (ROWS, ROWS), 0)
    columns = lax.broadcasted_iota(jnp.int32, (ROWS, ROWS), 1)
    return ((rows & 7) == (columns & 7)).astype(F32)


def rotation_tables():
    row = np.arange(ROWS)
    frame = ((row // 16) % 4) * 4 + (row // 64) * 2 + (row // 8) % 2
    half = HEAD // 2
    frequency = np.exp(np.arange(half) * (-2.0 * math.log(10000.0) / HEAD))
    angle = frame[:, None] * frequency[None, :]
    cosine = np.zeros((ROWS, 128), np.float32)
    sine = np.zeros((ROWS, 128), np.float32)
    cosine[:, :half] = cosine[:, half:HEAD] = np.cos(angle)
    sine[:, :half] = -np.sin(angle)
    sine[:, half:HEAD] = np.sin(angle)
    return cosine, sine


def prologue_kernel(place, *refs):
    sources, outs, held = refs[:4], refs[4:7], refs[7:11]
    modded, part, first_part, rest, sems = refs[11:]
    start = copier(sems)
    arrivals = [start(a, b) for a, b in zip(sources, held)]
    latents, modulation, qkv, out = held
    arrivals[0].wait()
    arrivals[1].wait()
    normed, _ = normalise(latents[...].astype(F32))
    modded[...] = (normed * (1.0 + modulation[1, 0:1]) + modulation[0, 0:1]).astype(BF16)
    finish = [start(modded, outs[0])]
    rest[...] = jnp.zeros_like(rest)
    arrivals[2].wait()
    arrivals[3].wait()
    for head in range(HEADS):

        @pl.when(place[0] == head)
        def _():
            for k in range(3):
                begin = k * FEATURES + head * HEAD
                both = qkv[:, :, begin : begin + HEAD].astype(F32)
                rest[0, :, k * HEAD : k * HEAD + HEAD] = both[:, 0]
                rest[1, :, k * HEAD : k * HEAD + HEAD] = both[:, 1]
            main = out[:, :, 128 * head : 128 * head + 128].astype(F32)
            tail = out[:, :, 1024 + 16 * head : 1040 + 16 * head].astype(F32)
            for block in range(2):
                rows = slice(18 * block, 18 * block + 18)
                rest[1, rows, 216:232] = tail[:, block]
                rest[1, rows, 256:384] = main[:, block]

    first = rest[0, :, :256].astype(BF16)
    tiles = jnp.concatenate([rest[1, :, 128 * t : 128 * t + 128] for t in range(3)], 0)
    mine = jnp.where(place[1] == 0, tiles[:54], tiles[54:])
    mine = jnp.concatenate([mine, jnp.zeros((2, 128), F32)], 0).astype(BF16)
    for copy in range(32):
        part[copy] = mine
        first_part[copy, :36] = first
        first_part[copy, 36:] = jnp.zeros((4, 256), BF16)
    finish += [start(part, outs[1]), start(first_part, outs[2])]
    for copy in finish:
        copy.wait()


def prologue(place, *operands):
    outs = (
        jax.ShapeDtypeStruct((ROWS, WIDTH), BF16),
        jax.ShapeDtypeStruct((32, 56, 128), BF16),
        jax.ShapeDtypeStruct((32, 40, 256), BF16),
    )
    return call(
        prologue_kernel,
        outs,
        [like(v) for v in operands]
        + [like(v) for v in outs]
        + [pltpu.VMEM((2, 36, 384), F32), pltpu.SemaphoreType.DMA((7,))],
        [SMEM] + [HBM] * 4,
        limit=60,
        out_space=pltpu.HBM,
    )(place, *operands)


def adapters_kernel(down, up, down_parts, up_parts):
    for block in range(2):
        high, low = halves(down[block])
        down_parts[block, :64] = high
        down_parts[block, 64:] = low
        for head in range(HEADS):
            start = head * HEAD
            columns = [up[block, :, k * FEATURES + start : k * FEATURES + start + HEAD] for k in range(3)]
            zero = jnp.zeros((RANK, 128 - HEAD), F32)
            wide = join_heads(*[jnp.concatenate([part, zero], 1) for part in columns])
            high, low = halves(wide)
            up_parts[block, head, :64] = high
            up_parts[block, head, 64:128] = low
            up_parts[block, head, 128:] = high


def adapters(down, up):
    return call(
        adapters_kernel,
        (
            jax.ShapeDtypeStruct((2, 128, WIDTH), BF16),
            jax.ShapeDtypeStruct((2, HEADS, 192, 256), BF16),
        ),
    )(down, up)


def spatial_kernel(
    place,
    modded,
    weight,
    down,
    up,
    latents,
    targets,
    sent,
    projected,
    reduced,
    weights,
    merged,
):
    for chunk in range(32):
        merged[36 * chunk : 36 * chunk + 36, :] = weight[chunk, :36]
    sent[:, :, 640 : 640 + WIDTH] = latents[...].astype(F32).reshape(16, 8, WIDTH).astype(BF16)
    sent[:, :, 640 + WIDTH :] = targets[...].astype(F32).reshape(16, 8, WIDTH).astype(BF16)
    sent[:, :, FEATURES:640] = jnp.zeros((16, 8, 640 - FEATURES), BF16)
    rows = modded[...].reshape(8 * ROWS, WIDTH)
    low = dot(rows, down[0], NT)
    high, rest = halves(low[:, :64] + low[:, 64:])
    reduced[...] = jnp.concatenate([high, rest], 1)
    adapted = dot(jnp.concatenate([high, high, rest], 1), up[0, place[0]])
    projected[...] = dot(rows, merged[...]) + adapted
    for frame in range(8):
        q, k, v = split_heads(projected[frame * ROWS : frame * ROWS + ROWS])
        q = (q * head_rate(q)).astype(BF16)
        k = (k * head_rate(k)).astype(BF16)
        w = softmax(dot(q, k, NT), None)
        weights[frame] = w
        attended = dot(w.astype(BF16), v.astype(BF16)).reshape(16, 8, 128)
        sent[:, :, HEAD * frame : HEAD * frame + HEAD] = attended[:, :, :HEAD].astype(BF16)


def spatial(place, *operands):
    return call(
        spatial_kernel,
        (
            jax.ShapeDtypeStruct((16, 8, 640 + 2 * WIDTH), BF16),
            jax.ShapeDtypeStruct((8 * ROWS, 256), F32),
            jax.ShapeDtypeStruct((8 * ROWS, 128), BF16),
            jax.ShapeDtypeStruct((8, ROWS, ROWS), F32),
        ),
        [pltpu.VMEM((WIDTH, 256), BF16)],
        [SMEM] + [VMEM] * 6,
        us=8,
    )(place, *operands)


def spatial_back_kernel(
    place, cotangent, up, modded, projected, reduced, weights, grad, d_projected
):
    for pair in range(4):
        rows = cotangent[:, 16 * pair : 16 * pair + 16, :].astype(F32).reshape(16, 2, 8, 128)
        for side in range(2):
            frame = 2 * pair + side
            span = slice(frame * ROWS, frame * ROWS + ROWS)
            q, k, v = split_heads(projected[span])
            q_out = (q * head_rate(q)).astype(BF16)
            k_out = (k * head_rate(k)).astype(BF16)
            d_q, d_k, d_v = attention_back(
                weights[frame],
                q_out,
                k_out,
                v.astype(BF16),
                rows[:, side].reshape(ROWS, 128).astype(BF16),
            )
            d_projected[span] = join_heads(head_norm_back(q, d_q), head_norm_back(k, d_k), d_v)
    high, rest = halves(d_projected[...])
    both = dot(reduced[...], jnp.concatenate([high, rest], 1), TN)
    grad_up = both[:64, :256] + both[64:, :256] + both[:64, 256:] + both[64:, 256:]
    head = up[0, place[0], :128]
    two = dot(high, head, NT) + dot(rest, head, NT)
    low_high, low_rest = halves(two[:, :64] + two[:, 64:])
    down = dot(
        jnp.concatenate([low_high, low_rest], 1), modded[...].reshape(8 * ROWS, WIDTH), TN
    )
    store_tiles(grad, 0, down[:64] + down[64:])
    store_tiles(grad, 9, grad_up)


def store_tiles(ref, start, values):
    for tile in range(values.shape[1] // 128):
        ref[:, start + tile, :] = values[:, 128 * tile : 128 * tile + 128]


def spatial_back(place, *operands):
    return call(
        spatial_back_kernel,
        jax.ShapeDtypeStruct((RANK, 11, 128), F32),
        [pltpu.VMEM((8 * ROWS, 256), F32)],
        [SMEM] + [VMEM] * 6,
        us=20,
    )(place, *operands)


def part_copies(gathered, held, sems):
    start = copier(sems)
    return [start(gathered.at[pl.ds(4 * x, 4)], held.at[pl.ds(4 * x, 4)]) for x in range(4)]


def assemble(copies, held, qkv, out_first, out_second):
    for x in range(4):
        copies[x].wait()
        for c in range(2):
            head = 2 * x + c
            lower, upper = held.at[4 * x + c], held.at[4 * x + 2 + c]
            main = slice(128 * head, 128 * head + 128)
            tail = slice(1024 + 16 * head, 1040 + 16 * head)
            for d in range(32):
                a = 36 * d
                qkv[head, a : a + 36, :128] = lower[d, 0:36]
                qkv[head, a : a + 18, 128:] = lower[d, 36:54]
                qkv[head, a + 18 : a + 36, 128:] = upper[d, 0:18]
                rows = slice(18 * d, 18 * d + 18)
                out_first[rows, main] = upper[d, 18:36]
                out_second[rows, main] = upper[d, 36:54]
                out_first[rows, tail] = lower[d, 36:54, 88:104]
                out_second[rows, tail] = upper[d, 0:18, 88:104]


def by_rows(received, columns):
    values = received[:, :, columns].astype(F32)
    frames = [x * 4 + l * 2 + c for l in range(2) for x in range(4) for c in range(2)]
    return jnp.concatenate([values[f] for f in frames], 0)


def temporal_kernel(
    received,
    modulation,
    gathered,
    down,
    up,
    cosine,
    sine,
    sent_out,
    grad_out,
    sent,
    grad,
    wide,
    modded,
    reduced,
    d_projected,
    ups,
    projected,
    weights,
    q_all,
    k_all,
    v_all,
    held,
    qkv,
    out_first,
    out_second,
    d_out,
    d_v,
    d_weights,
    d_scores,
    d_q,
    d_k,
    sems,
):
    copies = part_copies(gathered, held, sems)
    for head in range(HEADS):
        x, c = head // 2, head % 2
        rows = jnp.concatenate(
            [
                received[x * 4 + 2 * l + c, :, HEAD * g : HEAD * g + HEAD].astype(F32)
                for l in range(2)
                for g in range(8)
            ],
            0,
        )
        wide[:, HEAD * head : HEAD * head + HEAD] = rows
    assemble(copies, held, qkv, out_first, out_second)
    gate_first, gate_second = modulation[0, 2:3], modulation[1, 2:3]
    mixed = dot(wide[...].astype(BF16), out_first[...])
    middle = (by_rows(received, slice(640, 640 + WIDTH)) + gate_first * mixed).astype(BF16).astype(F32)
    normed, rate = normalise(middle)
    scale = 1.0 + modulation[1, 1:2]
    modded[...] = (normed * scale + modulation[1, 0:1]).astype(BF16)
    low = dot(modded[...], down[1], NT)
    high, rest = halves(low[:, :64] + low[:, 64:])
    reduced[...] = jnp.concatenate([high, rest], 1)
    three = jnp.concatenate([high, high, rest], 1)
    mask = same_token()
    for head in range(HEADS):
        projected[head] = dot(modded[...], qkv[head]) + dot(three, up[1, head])
    q, k, v = split_heads(projected[...].reshape(HEADS * ROWS, 256))
    q = (q * head_rate(q)).reshape(HEADS, ROWS, 128)
    k = (k * head_rate(k)).reshape(HEADS, ROWS, 128)
    q_all[...] = (q * cosine[...] + swap(q) * sine[...]).astype(BF16)
    k_all[...] = (k * cosine[...] + swap(k) * sine[...]).astype(BF16)
    v_all[...] = v.astype(BF16).reshape(HEADS, ROWS, 128)
    for head in range(HEADS):
        weights[head] = dot(q_all[head], k_all[head], NT)
    weights[...] = softmax(weights[...], mask)
    for head in range(HEADS):
        wide[:, HEAD * head : HEAD * head + HEAD] = dot(weights[head].astype(BF16), v_all[head])[:, :HEAD]
    mixed = dot(wide[...].astype(BF16), out_second[...])
    produced = (middle + gate_second * mixed).astype(BF16).astype(F32)
    error = ((produced - by_rows(received, slice(640 + WIDTH, None))) / WIDTH).astype(BF16).astype(F32)
    wide[...] = dot((gate_second * error).astype(BF16), out_second[...], NT)
    for head in range(HEADS):
        cotangent = wide[:, HEAD * head : HEAD * head + HEAD].astype(BF16)
        d_out[head] = jnp.concatenate([cotangent, jnp.zeros((ROWS, 128 - HEAD), BF16)], 1)
    for head in range(HEADS):
        d_v[head] = dot(weights[head].astype(BF16), d_out[head], TN)
        d_weights[head] = dot(d_out[head], v_all[head], NT)
    inner = d_weights[...].astype(BF16).astype(F32)
    inner = weights[...] * (inner - jnp.sum(inner * weights[...], -1, keepdims=True))
    d_scores[...] = (inner * SCALE).astype(BF16)
    for head in range(HEADS):
        d_q[head] = dot(d_scores[head], k_all[head])
        d_k[head] = dot(d_scores[head], q_all[head], TN)
    back = []
    q, k, _ = split_heads(projected[...].reshape(HEADS * ROWS, 256))
    for values, ref in ((q, d_q), (k, d_k)):
        d = ref[...].astype(BF16).astype(F32)
        d = (d * cosine[...] - swap(d) * sine[...]).reshape(HEADS * ROWS, 128)
        back.append(head_norm_back(values, d))
    d_val = d_v[...].astype(BF16).astype(F32).reshape(HEADS * ROWS, 128)
    d_projected[...] = join_heads(*back, d_val).reshape(HEADS, ROWS, 256)
    d_low = jnp.zeros((ROWS, 128), F32)
    d_modded = jnp.zeros((ROWS, WIDTH), F32)
    for head in range(HEADS):
        high, rest = halves(d_projected[head])
        d_low += dot(high, up[1, head, :128], NT) + dot(rest, up[1, head, :128], NT)
        d_modded += dot(high, qkv[head], NT)
    d_low = d_low[:, :64] + d_low[:, 64:]
    high, rest = halves(d_low)
    d_reduced = jnp.concatenate([high, rest], 1)
    through = dot(jnp.concatenate([high, high], 1), down[1]) + dot(rest, down[1, :64])
    d_modded = (d_modded.astype(BF16) + through.astype(BF16)).astype(F32)
    d_normed = d_modded * scale
    inner = jnp.mean(d_normed * normed, -1, keepdims=True)
    d_middle = rate * (d_normed - jnp.mean(d_normed, -1, keepdims=True) - normed * inner)
    d_middle = (error.astype(BF16) + d_middle.astype(BF16)).astype(F32)
    wide[...] = dot((gate_first * d_middle).astype(BF16), out_first[...], NT)
    for head in range(HEADS):
        x, c = head // 2, head % 2
        rows = wide[:, HEAD * head : HEAD * head + HEAD].astype(BF16)
        rows = jnp.concatenate([rows, jnp.zeros((ROWS, 128 - HEAD), BF16)], 1)
        sent[x * 4 + c] = rows[:64]
        sent[x * 4 + 2 + c] = rows[64:]
    start = copier(sems)
    sent_copy = start(sent, sent_out)
    ups[:, 1664:] = jnp.zeros((64, 128), F32)
    for head in range(HEADS):
        high, rest = halves(d_projected[head])
        both = dot(reduced[...], jnp.concatenate([high, rest], 1), TN)
        part = both[:64, :256] + both[64:, :256] + both[:64, 256:] + both[64:, 256:]
        for k in range(3):
            begin = k * FEATURES + head * HEAD
            ups[:, begin : begin + HEAD] = part[:, k * HEAD : k * HEAD + HEAD]
    down = dot(d_reduced, modded[...], TN)
    store_tiles(grad, 0, down[:64] + down[64:])
    store_tiles(grad, 9, ups[...])
    start(grad, grad_out).wait()
    sent_copy.wait()


def temporal(*operands):
    return call(
        temporal_kernel,
        (
            jax.ShapeDtypeStruct((16, 64, 128), BF16),
            jax.ShapeDtypeStruct((RANK, 23, 128), F32),
        ),
        [
            pltpu.VMEM((16, 64, 128), BF16),
            pltpu.VMEM((RANK, 23, 128), F32),
            pltpu.VMEM((ROWS, FEATURES), F32),
            pltpu.VMEM((ROWS, WIDTH), BF16),
            pltpu.VMEM((ROWS, 128), BF16),
            pltpu.VMEM((HEADS, ROWS, 256), F32),
            pltpu.VMEM((RANK, 1792), F32),
            pltpu.VMEM((HEADS, ROWS, 256), F32),
            pltpu.VMEM((HEADS, ROWS, ROWS), F32),
            pltpu.VMEM((HEADS, ROWS, 128), BF16),
            pltpu.VMEM((HEADS, ROWS, 128), BF16),
            pltpu.VMEM((HEADS, ROWS, 128), BF16),
            pltpu.VMEM((16, 32, 56, 128), BF16),
            pltpu.VMEM((HEADS, WIDTH, 256), BF16),
            pltpu.VMEM((FEATURES, WIDTH), BF16),
            pltpu.VMEM((FEATURES, WIDTH), BF16),
            pltpu.VMEM((HEADS, ROWS, 128), BF16),
            pltpu.VMEM((HEADS, ROWS, 128), F32),
            pltpu.VMEM((HEADS, ROWS, ROWS), F32),
            pltpu.VMEM((HEADS, ROWS, ROWS), BF16),
            pltpu.VMEM((HEADS, ROWS, 128), F32),
            pltpu.VMEM((HEADS, ROWS, 128), F32),
            pltpu.SemaphoreType.DMA((4,)),
        ],
        [VMEM] * 2 + [HBM] + [VMEM] * 4,
        limit=60,
        out_space=pltpu.HBM,
        us=25,
    )(*operands)


def epilogue_kernel(place, own, other, grad_down, grad_up):
    for side, ref in enumerate((own, other)):
        core = place[2] if side == 0 else 1 - place[2]
        rows = pl.ds(pl.multiple_of(core * 32, 32), 32)
        for tile in range(9):
            columns = slice(128 * tile, 128 * tile + 128)
            grad_down[0, rows, columns] = ref[:, tile, :]
            grad_down[1, rows, columns] = ref[:, 25 + tile, :]
        for head in range(HEADS):
            both = jnp.concatenate([ref[:, 9 + 2 * head, :], ref[:, 10 + 2 * head, :]], 1)
            for k in range(3):
                start = k * FEATURES + head * HEAD
                grad_up[0, rows, start : start + HEAD] = both[:, k * HEAD : k * HEAD + HEAD]
        for tile in range(13):
            grad_up[1, rows, 128 * tile : 128 * tile + 128] = ref[:, 34 + tile, :]
        grad_up[1, rows, 1664:1728] = ref[:, 47, :][:, :64]


def epilogue(place, own, other):
    vmem = spec(pltpu.VMEM)
    return call(
        epilogue_kernel,
        (
            jax.ShapeDtypeStruct((2, RANK, WIDTH), F32),
            jax.ShapeDtypeStruct((2, RANK, 3 * FEATURES), F32),
        ),
        in_specs=[spec(pltpu.SMEM), vmem, vmem],
    )(place, own, other)


def exchange(values, axes):
    return lax.all_to_all(values, axes, 0, 0)


def spread(values, axes, count):
    return exchange(jnp.broadcast_to(values[None], (count,) + values.shape), axes)


def swap_cores(values):
    return lax.ppermute(values, "c", [(0, 1), (1, 0)])


def add_cores(values, c):
    mine = lax.dynamic_slice_in_dim(values, c * 32, 32, 0)
    return mine, swap_cores(lax.dynamic_slice_in_dim(values, (1 - c) * 32, 32, 0))


def on_device(latents, targets, modulation, qkv, out, down, up):
    x, l, c = lax.axis_index("x"), lax.axis_index("l"), lax.axis_index("c")
    place = jnp.stack([x * 2 + c, l, c]).astype(jnp.int32)
    modulation = modulation[0]
    modded, part, first = prologue(
        place,
        latents[0, 0],
        modulation.transpose(1, 0, 2),
        qkv.transpose(1, 0, 2),
        out.transpose(1, 0, 2),
    )
    modded = lax.all_gather(modded, ("x", "c"), axis=0, tiled=False)
    gathered = lax.all_gather(exchange(part, DP), SEQ, axis=0, tiled=False)
    first = exchange(first, DP)
    down_parts, up_parts = adapters(down.transpose(0, 2, 1), up)
    sent, projected, reduced, weights = spatial(
        place, modded, first, down_parts, up_parts, latents[0, 0], targets[0, 0]
    )
    received = exchange(sent, SEQ)
    cosine, sine = rotation_tables()
    sent, late = temporal(
        received,
        modulation,
        gathered,
        down_parts,
        up_parts,
        jnp.asarray(cosine),
        jnp.asarray(sine),
    )
    cotangent = exchange(sent, SEQ)
    late = sum(add_cores(late, c))
    early = spatial_back(place, cotangent, up_parts, modded, projected, reduced, weights)
    mine, other = add_cores(early, c)
    first_up, second_up = mine[:, 9:], other[:, 9:]
    total = jnp.concatenate(
        [
            mine[:, :9] + other[:, :9],
            jnp.where(c == 0, first_up, second_up),
            jnp.where(c == 0, second_up, first_up),
            late,
        ],
        1,
    )
    total = exchange(total.reshape(32, 9, 4, 128), ("z", "x")).reshape(32, 36, 128)
    ups = jnp.sum(total[:, 9:13].reshape(8, 4, 4, 128), 0).reshape(16, 128)
    total = jnp.concatenate([jnp.sum(total[:, :9], 0), ups, jnp.sum(total[:, 13:], 0)], 0)
    total = jnp.sum(spread(total, ("h", "l"), 8), 0)
    total = spread(total, ("z", "x"), 32)
    grad_down, grad_up = epilogue(place, total, swap_cores(total))
    return grad_down.transpose(0, 2, 1), grad_up


def solution(mesh):
    inner = Mesh(mesh.devices.reshape(8, 4, 4, 2, 2), ("z", "h", "x", "l", "c"))
    in_specs = (
        P(DP, SEQ, None, None),
        P(DP, SEQ, None, None),
        P(DP, None, None, None),
        P(None, DP, None),
        P(None, DP, None),
        P(),
        P(),
    )
    return jax.shard_map(
        on_device, mesh=inner, in_specs=in_specs, out_specs=(P(), P()), check_vma=False
    )
```

```python
import math

import jax
import jax.numpy as jnp
import numpy as np
from jax import lax
from jax.experimental import pallas as pl
from jax.experimental.pallas import tpu as pltpu
from jax.sharding import Mesh, PartitionSpec as P

WIDTH = 1152
HEADS = 8
HEAD = 72
RANK = 64
FEATURES = HEADS * HEAD
ROWS = 128
F32 = jnp.float32
BF16 = jnp.bfloat16
SCALE = 1.0 / math.sqrt(HEAD)
MIB = 1 << 20
DP = ("z", "h")
SEQ = ("x", "l", "c")


def call(kernel, out_shape, scratch=(), in_specs=None, limit=20, out_space=pltpu.VMEM, us=2):
    vmem = pl.BlockSpec(memory_space=pltpu.VMEM)
    out_spec = pl.BlockSpec(memory_space=out_space)

    def run(*operands):
        return pl.pallas_call(
            kernel,
            out_shape=out_shape,
            in_specs=in_specs or [vmem] * len(operands),
            out_specs=jax.tree.map(lambda _: out_spec, out_shape),
            scratch_shapes=list(scratch),
            compiler_params=pltpu.CompilerParams(vmem_limit_bytes=limit * MIB),
            cost_estimate=pl.CostEstimate(
                flops=us * 10**9, bytes_accessed=us * 3 * 10**6, transcendentals=0
            ),
        )(*operands)

    return run


def spec(space):
    return pl.BlockSpec(memory_space=space)


SMEM, VMEM, HBM = spec(pltpu.SMEM), spec(pltpu.VMEM), spec(pltpu.HBM)


def copier(sems):
    count = iter(range(100))

    def start(source, target):
        copy = pltpu.make_async_copy(source, target, sems.at[next(count)])
        copy.start()
        return copy

    return start


def like(values):
    return pltpu.VMEM(values.shape, values.dtype)


def dot(a, b, dims=((1,), (0,))):
    return lax.dot_general(a, b, (dims, ((), ())), preferred_element_type=F32)


NT = ((1,), (1,))
TN = ((0,), (0,))


def halves(values):
    high = values.astype(BF16)
    return high, (values - high.astype(F32)).astype(BF16)


def normalise(values):
    centred = values - jnp.mean(values, -1, keepdims=True)
    rate = lax.rsqrt(jnp.mean(centred * centred, -1, keepdims=True) + 1e-06)
    return centred * rate, rate


def lane_mask(width, dtype=F32):
    lanes = lax.broadcasted_iota(jnp.int32, (1, 128), 1)
    return (lanes < width).astype(dtype)


def split_heads(projected):
    keep = lane_mask(HEAD)
    q = projected[:, :128] * keep
    k = pltpu.roll(projected, 256 - HEAD, 1)[:, :128] * keep
    v = pltpu.roll(projected, 256 - 2 * HEAD, 1)[:, :128] * keep
    return q, k, v


def join_heads(q, k, v):
    zero = jnp.zeros_like(q)
    return (
        jnp.concatenate([q, zero], 1)
        + pltpu.roll(jnp.concatenate([k, zero], 1), HEAD, 1)
        + pltpu.roll(jnp.concatenate([v, zero], 1), 2 * HEAD, 1)
    )


def head_rate(values):
    return lax.rsqrt(jnp.sum(values * values, -1, keepdims=True) * (1.0 / HEAD) + 1e-06)


def head_norm_back(values, cotangent):
    rate = head_rate(values)
    inner = jnp.sum(cotangent * values, -1, keepdims=True) * (1.0 / HEAD)
    return rate * (cotangent - values * (rate * rate * inner))


def swap(values):
    lanes = lax.broadcasted_iota(jnp.int32, (1, 128), 1)
    return jnp.where(
        lanes < HEAD // 2,
        pltpu.roll(values, 128 - HEAD // 2, values.ndim - 1),
        pltpu.roll(values, HEAD // 2, values.ndim - 1),
    )


def softmax(scores, mask):
    weights = jnp.exp(scores * SCALE)
    if mask is not None:
        weights = weights * mask
    return weights / jnp.sum(weights, -1, keepdims=True)


def attention_back(weights, q, k, v, cotangent):
    rounded = weights.astype(BF16)
    d_v = dot(rounded, cotangent, TN).astype(BF16)
    d_weights = dot(cotangent, v, NT).astype(BF16).astype(F32)
    d_scores = weights * (d_weights - jnp.sum(d_weights * weights, -1, keepdims=True))
    d_scores = (d_scores * SCALE).astype(BF16)
    d_q = dot(d_scores, k).astype(BF16)
    d_k = dot(d_scores, q, TN).astype(BF16)
    return d_q.astype(F32), d_k.astype(F32), d_v.astype(F32)


def same_token():
    rows = lax.broadcasted_iota(jnp.int32, (ROWS, ROWS), 0)
    columns = lax.broadcasted_iota(jnp.int32, (ROWS, ROWS), 1)
    return ((rows & 7) == (columns & 7)).astype(F32)


def rotation_tables():
    row = np.arange(ROWS)
    frame = ((row // 16) % 4) * 4 + (row // 64) * 2 + (row // 8) % 2
    half = HEAD // 2
    frequency = np.exp(np.arange(half) * (-2.0 * math.log(10000.0) / HEAD))
    angle = frame[:, None] * frequency[None, :]
    cosine = np.zeros((ROWS, 128), np.float32)
    sine = np.zeros((ROWS, 128), np.float32)
    cosine[:, :half] = cosine[:, half:HEAD] = np.cos(angle)
    sine[:, :half] = -np.sin(angle)
    sine[:, half:HEAD] = np.sin(angle)
    return cosine, sine


def prologue_kernel(place, *refs):
    sources, outs, held = refs[:4], refs[4:7], refs[7:11]
    modded, part, first_part, rest, sems = refs[11:]
    start = copier(sems)
    arrivals = [start(a, b) for a, b in zip(sources, held)]
    latents, modulation, qkv, out = held
    arrivals[0].wait()
    arrivals[1].wait()
    normed, _ = normalise(latents[...].astype(F32))
    modded[...] = (normed * (1.0 + modulation[1, 0:1]) + modulation[0, 0:1]).astype(BF16)
    finish = [start(modded, outs[0])]
    rest[...] = jnp.zeros_like(rest)
    arrivals[2].wait()
    arrivals[3].wait()
    for head in range(HEADS):

        @pl.when(place[0] == head)
        def _():
            for k in range(3):
                begin = k * FEATURES + head * HEAD
                both = qkv[:, :, begin : begin + HEAD].astype(F32)
                rest[0, :, k * HEAD : k * HEAD + HEAD] = both[:, 0]
                rest[1, :, k * HEAD : k * HEAD + HEAD] = both[:, 1]
            main = out[:, :, 128 * head : 128 * head + 128].astype(F32)
            tail = out[:, :, 1024 + 16 * head : 1040 + 16 * head].astype(F32)
            for block in range(2):
                rows = slice(18 * block, 18 * block + 18)
                rest[1, rows, 216:232] = tail[:, block]
                rest[1, rows, 256:384] = main[:, block]

    first = jnp.concatenate([rest[0, :, :128], rest[0, :, 128:256]], 0).astype(BF16)
    tiles = jnp.concatenate([rest[1, :, 128 * t : 128 * t + 128] for t in range(3)], 0)
    mine = jnp.where(place[1] == 0, tiles[:54], tiles[54:])
    mine = jnp.concatenate([mine, jnp.zeros((2, 128), F32)], 0).astype(BF16)
    for copy in range(32):
        part[copy] = mine
        first_part[copy] = first
    finish += [start(part, outs[1]), start(first_part, outs[2])]
    for copy in finish:
        copy.wait()


def prologue(place, *operands):
    outs = (
        jax.ShapeDtypeStruct((ROWS, WIDTH), BF16),
        jax.ShapeDtypeStruct((32, 56, 128), BF16),
        jax.ShapeDtypeStruct((32, 72, 128), BF16),
    )
    return call(
        prologue_kernel,
        outs,
        [like(v) for v in operands]
        + [like(v) for v in outs]
        + [pltpu.VMEM((2, 36, 384), F32), pltpu.SemaphoreType.DMA((7,))],
        [SMEM] + [HBM] * 4,
        limit=60,
        out_space=pltpu.HBM,
    )(place, *operands)


def adapters_kernel(place, down, up, down_first, down_second, up_first, up_second, held):
    for block in range(2):
        high, low = halves(down[block])
        down_parts = down_second if block else down_first
        down_parts[:64] = high
        down_parts[64:] = low
        for head in range(HEADS):
            start = head * HEAD
            columns = [up[block, :, k * FEATURES + start : k * FEATURES + start + HEAD] for k in range(3)]
            zero = jnp.zeros((RANK, 128 - HEAD), F32)
            wide = join_heads(*[jnp.concatenate([part, zero], 1) for part in columns])
            high, low = halves(wide)
            parts = jnp.concatenate([high, low, high], 0)
            if block == 0:
                held[head] = parts
            else:
                up_second[head] = parts
    up_first[...] = held[place[0]]


def adapters(place, down, up):
    return call(
        adapters_kernel,
        (
            jax.ShapeDtypeStruct((128, WIDTH), BF16),
            jax.ShapeDtypeStruct((128, WIDTH), BF16),
            jax.ShapeDtypeStruct((192, 256), BF16),
            jax.ShapeDtypeStruct((HEADS, 192, 256), BF16),
        ),
        [pltpu.VMEM((HEADS, 192, 256), BF16)],
        [SMEM, VMEM, VMEM],
    )(place, down, up)


def spatial_kernel(
    modded,
    weight,
    down,
    up,
    latents,
    targets,
    sent,
    projected,
    reduced,
    weights,
    merged,
):
    for chunk in range(32):
        rows = slice(36 * chunk, 36 * chunk + 36)
        merged[rows, :128] = weight[chunk, :36]
        merged[rows, 128:] = weight[chunk, 36:]
    sent[:, :, 640 : 640 + WIDTH] = latents[...].astype(F32).reshape(16, 8, WIDTH).astype(BF16)
    sent[:, :, 640 + WIDTH :] = targets[...].astype(F32).reshape(16, 8, WIDTH).astype(BF16)
    sent[:, :, FEATURES:640] = jnp.zeros((16, 8, 640 - FEATURES), BF16)
    rows = modded[...].reshape(8 * ROWS, WIDTH)
    low = dot(rows, down[...], NT)
    high, rest = halves(low[:, :64] + low[:, 64:])
    reduced[...] = jnp.concatenate([high, rest], 1)
    adapted = dot(jnp.concatenate([high, high, rest], 1), up[...])
    projected[...] = dot(rows, merged[...]) + adapted
    for frame in range(8):
        q, k, v = split_heads(projected[frame * ROWS : frame * ROWS + ROWS])
        q = (q * head_rate(q)).astype(BF16)
        k = (k * head_rate(k)).astype(BF16)
        w = softmax(dot(q, k, NT), None)
        weights[frame] = w
        attended = dot(w.astype(BF16), v.astype(BF16)).reshape(16, 8, 128)
        sent[:, :, HEAD * frame : HEAD * frame + HEAD] = attended[:, :, :HEAD].astype(BF16)


def spatial(*operands):
    return call(
        spatial_kernel,
        (
            jax.ShapeDtypeStruct((16, 8, 640 + 2 * WIDTH), BF16),
            jax.ShapeDtypeStruct((8 * ROWS, 256), F32),
            jax.ShapeDtypeStruct((8 * ROWS, 128), BF16),
            jax.ShapeDtypeStruct((8, ROWS, ROWS), F32),
        ),
        [pltpu.VMEM((WIDTH, 256), BF16)],
        us=8,
    )(*operands)


def spatial_back_kernel(
    cotangent, up, modded, projected, reduced, weights, grad, d_projected
):
    for pair in range(4):
        rows = cotangent[:, 16 * pair : 16 * pair + 16, :].astype(F32).reshape(16, 2, 8, 128)
        for side in range(2):
            frame = 2 * pair + side
            span = slice(frame * ROWS, frame * ROWS + ROWS)
            q, k, v = split_heads(projected[span])
            q_out = (q * head_rate(q)).astype(BF16)
            k_out = (k * head_rate(k)).astype(BF16)
            d_q, d_k, d_v = attention_back(
                weights[frame],
                q_out,
                k_out,
                v.astype(BF16),
                rows[:, side].reshape(ROWS, 128).astype(BF16),
            )
            d_projected[span] = join_heads(head_norm_back(q, d_q), head_norm_back(k, d_k), d_v)
    high, rest = halves(d_projected[...])
    both = dot(reduced[...], jnp.concatenate([high, rest], 1), TN)
    grad_up = both[:64, :256] + both[64:, :256] + both[:64, 256:] + both[64:, 256:]
    head = up[:128]
    two = dot(high, head, NT) + dot(rest, head, NT)
    low_high, low_rest = halves(two[:, :64] + two[:, 64:])
    down = dot(
        jnp.concatenate([low_high, low_rest], 1), modded[...].reshape(8 * ROWS, WIDTH), TN
    )
    store_tiles(grad, 0, down[:64] + down[64:])
    store_tiles(grad, 9, grad_up)


def store_tiles(ref, start, values):
    for tile in range(values.shape[1] // 128):
        ref[:, start + tile, :] = values[:, 128 * tile : 128 * tile + 128]


def spatial_back(*operands):
    return call(
        spatial_back_kernel,
        jax.ShapeDtypeStruct((RANK, 11, 128), F32),
        [pltpu.VMEM((8 * ROWS, 256), F32)],
        us=20,
    )(*operands)


def part_copies(gathered, held, start):
    return [start(gathered.at[pl.ds(4 * x, 4)], held.at[pl.ds(4 * x, 4)]) for x in range(4)]


def assemble(copies, held, qkv, out_first, out_second):
    for x in range(4):
        copies[x].wait()
        for c in range(2):
            head = 2 * x + c
            lower, upper = held.at[4 * x + c], held.at[4 * x + 2 + c]
            main = slice(128 * head, 128 * head + 128)
            tail = slice(1024 + 16 * head, 1040 + 16 * head)
            for d in range(32):
                a = 36 * d
                qkv[head, a : a + 36, :128] = lower[d, 0:36]
                qkv[head, a : a + 18, 128:] = lower[d, 36:54]
                qkv[head, a + 18 : a + 36, 128:] = upper[d, 0:18]
                rows = slice(18 * d, 18 * d + 18)
                out_first[rows, main] = upper[d, 18:36]
                out_second[rows, main] = upper[d, 36:54]
                out_first[rows, tail] = lower[d, 36:54, 88:104]
                out_second[rows, tail] = upper[d, 0:18, 88:104]


def by_rows(received, columns):
    values = received[:, :, columns].astype(F32)
    frames = [x * 4 + l * 2 + c for l in range(2) for x in range(4) for c in range(2)]
    return jnp.concatenate([values[f] for f in frames], 0)


def temporal_kernel(
    gathered,
    received_in,
    modulation_in,
    down_in,
    up_in,
    cosine_in,
    sine_in,
    sent_out,
    grad_out,
    received,
    modulation,
    down,
    up,
    cosine,
    sine,
    sent,
    grad,
    wide,
    modded,
    reduced,
    d_projected,
    ups,
    projected,
    weights,
    q_all,
    k_all,
    v_all,
    held,
    qkv,
    out_first,
    out_second,
    d_out,
    d_v,
    d_weights,
    d_scores,
    d_q,
    d_k,
    sems,
):
    start = copier(sems)
    copies = part_copies(gathered, held, start)
    arrivals = [
        start(received_in, received),
        start(modulation_in, modulation),
        start(down_in, down),
        start(up_in, up),
        start(cosine_in, cosine),
        start(sine_in, sine),
    ]
    assemble(copies, held, qkv, out_first, out_second)
    for copy in arrivals:
        copy.wait()
    for head in range(HEADS):
        x, c = head // 2, head % 2
        rows = jnp.concatenate(
            [
                received[x * 4 + 2 * l + c, :, HEAD * g : HEAD * g + HEAD].astype(F32)
                for l in range(2)
                for g in range(8)
            ],
            0,
        )
        wide[:, HEAD * head : HEAD * head + HEAD] = rows
    gate_first, gate_second = modulation[2, 0:1], modulation[2, 1:2]
    mixed = dot(wide[...].astype(BF16), out_first[...])
    middle = (by_rows(received, slice(640, 640 + WIDTH)) + gate_first * mixed).astype(BF16).astype(F32)
    normed, rate = normalise(middle)
    scale = 1.0 + modulation[1, 1:2]
    modded[...] = (normed * scale + modulation[0, 1:2]).astype(BF16)
    low = dot(modded[...], down[...], NT)
    high, rest = halves(low[:, :64] + low[:, 64:])
    reduced[...] = jnp.concatenate([high, rest], 1)
    three = jnp.concatenate([high, high, rest], 1)
    mask = same_token()
    for head in range(HEADS):
        projected[head] = dot(modded[...], qkv[head]) + dot(three, up[head])
    q, k, v = split_heads(projected[...].reshape(HEADS * ROWS, 256))
    q = (q * head_rate(q)).reshape(HEADS, ROWS, 128)
    k = (k * head_rate(k)).reshape(HEADS, ROWS, 128)
    q_all[...] = (q * cosine[...] + swap(q) * sine[...]).astype(BF16)
    k_all[...] = (k * cosine[...] + swap(k) * sine[...]).astype(BF16)
    v_all[...] = v.astype(BF16).reshape(HEADS, ROWS, 128)
    for head in range(HEADS):
        weights[head] = dot(q_all[head], k_all[head], NT)
    weights[...] = softmax(weights[...], mask)
    for head in range(HEADS):
        wide[:, HEAD * head : HEAD * head + HEAD] = dot(weights[head].astype(BF16), v_all[head])[:, :HEAD]
    mixed = dot(wide[...].astype(BF16), out_second[...])
    produced = (middle + gate_second * mixed).astype(BF16).astype(F32)
    error = ((produced - by_rows(received, slice(640 + WIDTH, None))) / WIDTH).astype(BF16).astype(F32)
    wide[...] = dot((gate_second * error).astype(BF16), out_second[...], NT)
    for head in range(HEADS):
        cotangent = wide[:, HEAD * head : HEAD * head + HEAD].astype(BF16)
        d_out[head] = jnp.concatenate([cotangent, jnp.zeros((ROWS, 128 - HEAD), BF16)], 1)
    for head in range(HEADS):
        d_v[head] = dot(weights[head].astype(BF16), d_out[head], TN)
        d_weights[head] = dot(d_out[head], v_all[head], NT)
    inner = d_weights[...].astype(BF16).astype(F32)
    inner = weights[...] * (inner - jnp.sum(inner * weights[...], -1, keepdims=True))
    d_scores[...] = (inner * SCALE).astype(BF16)
    for head in range(HEADS):
        d_q[head] = dot(d_scores[head], k_all[head])
        d_k[head] = dot(d_scores[head], q_all[head], TN)
    back = []
    q, k, _ = split_heads(projected[...].reshape(HEADS * ROWS, 256))
    for values, ref in ((q, d_q), (k, d_k)):
        d = ref[...].astype(BF16).astype(F32)
        d = (d * cosine[...] - swap(d) * sine[...]).reshape(HEADS * ROWS, 128)
        back.append(head_norm_back(values, d))
    d_val = d_v[...].astype(BF16).astype(F32).reshape(HEADS * ROWS, 128)
    d_projected[...] = join_heads(*back, d_val).reshape(HEADS, ROWS, 256)
    d_low = jnp.zeros((ROWS, 128), F32)
    d_modded = jnp.zeros((ROWS, WIDTH), F32)
    for head in range(HEADS):
        high, rest = halves(d_projected[head])
        d_low += dot(high, up[head, :128], NT) + dot(rest, up[head, :128], NT)
        d_modded += dot(high, qkv[head], NT)
    d_low = d_low[:, :64] + d_low[:, 64:]
    high, rest = halves(d_low)
    d_reduced = jnp.concatenate([high, rest], 1)
    through = dot(jnp.concatenate([high, high], 1), down[...]) + dot(rest, down[:64])
    d_modded = (d_modded.astype(BF16) + through.astype(BF16)).astype(F32)
    d_normed = d_modded * scale
    inner = jnp.mean(d_normed * normed, -1, keepdims=True)
    d_middle = rate * (d_normed - jnp.mean(d_normed, -1, keepdims=True) - normed * inner)
    d_middle = (error.astype(BF16) + d_middle.astype(BF16)).astype(F32)
    wide[...] = dot((gate_first * d_middle).astype(BF16), out_first[...], NT)
    for head in range(HEADS):
        x, c = head // 2, head % 2
        rows = wide[:, HEAD * head : HEAD * head + HEAD].astype(BF16)
        rows = jnp.concatenate([rows, jnp.zeros((ROWS, 128 - HEAD), BF16)], 1)
        sent[x * 4 + c] = rows[:64]
        sent[x * 4 + 2 + c] = rows[64:]
    sent_copy = start(sent, sent_out)
    ups[:, 1664:] = jnp.zeros((64, 128), F32)
    for head in range(HEADS):
        high, rest = halves(d_projected[head])
        both = dot(reduced[...], jnp.concatenate([high, rest], 1), TN)
        part = both[:64, :256] + both[64:, :256] + both[:64, 256:] + both[64:, 256:]
        for k in range(3):
            begin = k * FEATURES + head * HEAD
            ups[:, begin : begin + HEAD] = part[:, k * HEAD : k * HEAD + HEAD]
    down = dot(d_reduced, modded[...], TN)
    store_tiles(grad, 0, down[:64] + down[64:])
    store_tiles(grad, 9, ups[...])
    start(grad, grad_out).wait()
    sent_copy.wait()


def temporal(gathered, *operands):
    return call(
        temporal_kernel,
        (
            jax.ShapeDtypeStruct((16, 64, 128), BF16),
            jax.ShapeDtypeStruct((RANK, 23, 128), F32),
        ),
        [like(v) for v in operands]
        + [
            pltpu.VMEM((16, 64, 128), BF16),
            pltpu.VMEM((RANK, 23, 128), F32),
            pltpu.VMEM((ROWS, FEATURES), F32),
            pltpu.VMEM((ROWS, WIDTH), BF16),
            pltpu.VMEM((ROWS, 128), BF16),
            pltpu.VMEM((HEADS, ROWS, 256), F32),
            pltpu.VMEM((RANK, 1792), F32),
            pltpu.VMEM((HEADS, ROWS, 256), F32),
            pltpu.VMEM((HEADS, ROWS, ROWS), F32),
            pltpu.VMEM((HEADS, ROWS, 128), BF16),
            pltpu.VMEM((HEADS, ROWS, 128), BF16),
            pltpu.VMEM((HEADS, ROWS, 128), BF16),
            pltpu.VMEM((16, 32, 56, 128), BF16),
            pltpu.VMEM((HEADS, WIDTH, 256), BF16),
            pltpu.VMEM((FEATURES, WIDTH), BF16),
            pltpu.VMEM((FEATURES, WIDTH), BF16),
            pltpu.VMEM((HEADS, ROWS, 128), BF16),
            pltpu.VMEM((HEADS, ROWS, 128), F32),
            pltpu.VMEM((HEADS, ROWS, ROWS), F32),
            pltpu.VMEM((HEADS, ROWS, ROWS), BF16),
            pltpu.VMEM((HEADS, ROWS, 128), F32),
            pltpu.VMEM((HEADS, ROWS, 128), F32),
            pltpu.SemaphoreType.DMA((12,)),
        ],
        [HBM] * 7,
        limit=60,
        out_space=pltpu.HBM,
        us=25,
    )(gathered, *operands)


def epilogue_kernel(place, own, other, grad_down, grad_up):
    for side, ref in enumerate((own, other)):
        core = place[2] if side == 0 else 1 - place[2]
        rows = pl.ds(pl.multiple_of(core * 32, 32), 32)
        for tile in range(9):
            columns = slice(128 * tile, 128 * tile + 128)
            grad_down[0, rows, columns] = ref[:, tile, :]
            grad_down[1, rows, columns] = ref[:, 25 + tile, :]
        for head in range(HEADS):
            both = jnp.concatenate([ref[:, 9 + 2 * head, :], ref[:, 10 + 2 * head, :]], 1)
            for k in range(3):
                start = k * FEATURES + head * HEAD
                grad_up[0, rows, start : start + HEAD] = both[:, k * HEAD : k * HEAD + HEAD]
        for tile in range(13):
            grad_up[1, rows, 128 * tile : 128 * tile + 128] = ref[:, 34 + tile, :]
        grad_up[1, rows, 1664:1728] = ref[:, 47, :][:, :64]


def epilogue(place, own, other):
    vmem = spec(pltpu.VMEM)
    return call(
        epilogue_kernel,
        (
            jax.ShapeDtypeStruct((2, RANK, WIDTH), F32),
            jax.ShapeDtypeStruct((2, RANK, 3 * FEATURES), F32),
        ),
        in_specs=[spec(pltpu.SMEM), vmem, vmem],
    )(place, own, other)


def exchange(values, axes):
    return lax.all_to_all(values, axes, 0, 0)


def spread(values, axes, count):
    return exchange(jnp.broadcast_to(values[None], (count,) + values.shape), axes)


def swap_cores(values):
    return lax.ppermute(values, "c", [(0, 1), (1, 0)])


def add_cores(values, c):
    mine = lax.dynamic_slice_in_dim(values, c * 32, 32, 0)
    return mine, swap_cores(lax.dynamic_slice_in_dim(values, (1 - c) * 32, 32, 0))


def on_device(latents, targets, modulation, qkv, out, down, up):
    x, l, c = lax.axis_index("x"), lax.axis_index("l"), lax.axis_index("c")
    place = jnp.stack([x * 2 + c, l, c]).astype(jnp.int32)
    modulation = modulation[0].transpose(1, 0, 2)
    modded, part, first = prologue(
        place,
        latents[0, 0],
        modulation,
        qkv.transpose(1, 0, 2),
        out.transpose(1, 0, 2),
    )
    modded = lax.all_gather(modded, ("x", "c"), axis=0, tiled=False)
    gathered = lax.all_gather(exchange(part, DP), SEQ, axis=0, tiled=False)
    first = exchange(first, DP)
    down_first, down_second, up_first, up_second = adapters(place, down.transpose(0, 2, 1), up)
    sent, projected, reduced, weights = spatial(
        modded, first, down_first, up_first, latents[0, 0], targets[0, 0]
    )
    received = exchange(sent, SEQ)
    cosine, sine = rotation_tables()
    sent, late = temporal(
        gathered,
        received,
        modulation,
        down_second,
        up_second,
        jnp.asarray(cosine),
        jnp.asarray(sine),
    )
    cotangent = exchange(sent, SEQ)
    late = sum(add_cores(late, c))
    early = spatial_back(cotangent, up_first, modded, projected, reduced, weights)
    mine, other = add_cores(early, c)
    first_up, second_up = mine[:, 9:], other[:, 9:]
    total = jnp.concatenate(
        [
            mine[:, :9] + other[:, :9],
            jnp.where(c == 0, first_up, second_up),
            jnp.where(c == 0, second_up, first_up),
            late,
        ],
        1,
    )
    total = exchange(total.reshape(32, 9, 4, 128), ("z", "x")).reshape(32, 36, 128)
    ups = jnp.sum(total[:, 9:13].reshape(8, 4, 4, 128), 0).reshape(16, 128)
    total = jnp.concatenate([jnp.sum(total[:, :9], 0), ups, jnp.sum(total[:, 13:], 0)], 0)
    total = jnp.sum(spread(total, ("h", "l"), 8), 0)
    total = spread(total, ("z", "x"), 32)
    grad_down, grad_up = epilogue(place, total, swap_cores(total))
    return grad_down.transpose(0, 2, 1), grad_up


def solution(mesh):
    inner = Mesh(mesh.devices.reshape(8, 4, 4, 2, 2), ("z", "h", "x", "l", "c"))
    in_specs = (
        P(DP, SEQ, None, None),
        P(DP, SEQ, None, None),
        P(DP, None, None, None),
        P(None, DP, None),
        P(None, DP, None),
        P(),
        P(),
    )
    return jax.shard_map(
        on_device, mesh=inner, in_specs=in_specs, out_specs=(P(), P()), check_vma=False
    )
```

```python
import math

import jax
import jax.numpy as jnp
import numpy as np
from jax import lax
from jax.experimental import pallas as pl
from jax.experimental.pallas import tpu as pltpu
from jax.sharding import Mesh, PartitionSpec as P

WIDTH = 1152
HEADS = 8
HEAD = 72
RANK = 64
FEATURES = HEADS * HEAD
ROWS = 128
F32 = jnp.float32
BF16 = jnp.bfloat16
SCALE = 1.0 / math.sqrt(HEAD)
MIB = 1 << 20
DP = ("z", "h")
SEQ = ("x", "l", "c")


def call(kernel, out_shape, scratch=(), in_specs=None, limit=20, out_space=pltpu.VMEM, us=2):
    vmem = pl.BlockSpec(memory_space=pltpu.VMEM)
    out_spec = pl.BlockSpec(memory_space=out_space)

    def run(*operands):
        return pl.pallas_call(
            kernel,
            out_shape=out_shape,
            in_specs=in_specs or [vmem] * len(operands),
            out_specs=jax.tree.map(lambda _: out_spec, out_shape),
            scratch_shapes=list(scratch),
            compiler_params=pltpu.CompilerParams(vmem_limit_bytes=limit * MIB),
            cost_estimate=pl.CostEstimate(
                flops=us * 10**9, bytes_accessed=us * 3 * 10**6, transcendentals=0
            ),
        )(*operands)

    return run


def spec(space):
    return pl.BlockSpec(memory_space=space)


SMEM, VMEM, HBM = spec(pltpu.SMEM), spec(pltpu.VMEM), spec(pltpu.HBM)


def copier(sems):
    count = iter(range(100))

    def start(source, target):
        copy = pltpu.make_async_copy(source, target, sems.at[next(count)])
        copy.start()
        return copy

    return start


def like(values):
    return pltpu.VMEM(values.shape, values.dtype)


def dot(a, b, dims=((1,), (0,))):
    return lax.dot_general(a, b, (dims, ((), ())), preferred_element_type=F32)


NT = ((1,), (1,))
TN = ((0,), (0,))


def halves(values):
    high = values.astype(BF16)
    return high, (values - high.astype(F32)).astype(BF16)


def normalise(values):
    centred = values - jnp.mean(values, -1, keepdims=True)
    rate = lax.rsqrt(jnp.mean(centred * centred, -1, keepdims=True) + 1e-06)
    return centred * rate, rate


def lane_mask(width, dtype=F32):
    lanes = lax.broadcasted_iota(jnp.int32, (1, 128), 1)
    return (lanes < width).astype(dtype)


def split_heads(projected):
    keep = lane_mask(HEAD)
    q = projected[:, :128] * keep
    k = pltpu.roll(projected, 256 - HEAD, 1)[:, :128] * keep
    v = pltpu.roll(projected, 256 - 2 * HEAD, 1)[:, :128] * keep
    return q, k, v


def join_heads(q, k, v):
    zero = jnp.zeros_like(q)
    return (
        jnp.concatenate([q, zero], 1)
        + pltpu.roll(jnp.concatenate([k, zero], 1), HEAD, 1)
        + pltpu.roll(jnp.concatenate([v, zero], 1), 2 * HEAD, 1)
    )


def head_rate(values):
    return lax.rsqrt(jnp.sum(values * values, -1, keepdims=True) * (1.0 / HEAD) + 1e-06)


def head_norm_back(values, cotangent):
    rate = head_rate(values)
    inner = jnp.sum(cotangent * values, -1, keepdims=True) * (1.0 / HEAD)
    return rate * (cotangent - values * (rate * rate * inner))


def swap(values):
    lanes = lax.broadcasted_iota(jnp.int32, (1, 128), 1)
    return jnp.where(
        lanes < HEAD // 2,
        pltpu.roll(values, 128 - HEAD // 2, values.ndim - 1),
        pltpu.roll(values, HEAD // 2, values.ndim - 1),
    )


def softmax(scores, mask):
    weights = jnp.exp(scores * SCALE)
    if mask is not None:
        weights = weights * mask
    return weights / jnp.sum(weights, -1, keepdims=True)


def attention_back(weights, q, k, v, cotangent):
    rounded = weights.astype(BF16)
    d_v = dot(rounded, cotangent, TN).astype(BF16)
    d_weights = dot(cotangent, v, NT).astype(BF16).astype(F32)
    d_scores = weights * (d_weights - jnp.sum(d_weights * weights, -1, keepdims=True))
    d_scores = (d_scores * SCALE).astype(BF16)
    d_q = dot(d_scores, k).astype(BF16)
    d_k = dot(d_scores, q, TN).astype(BF16)
    return d_q.astype(F32), d_k.astype(F32), d_v.astype(F32)


def same_token():
    rows = lax.broadcasted_iota(jnp.int32, (ROWS, ROWS), 0)
    columns = lax.broadcasted_iota(jnp.int32, (ROWS, ROWS), 1)
    return ((rows & 7) == (columns & 7)).astype(F32)


def rotation_tables():
    row = np.arange(ROWS)
    frame = ((row // 16) % 4) * 4 + (row // 64) * 2 + (row // 8) % 2
    half = HEAD // 2
    frequency = np.exp(np.arange(half) * (-2.0 * math.log(10000.0) / HEAD))
    angle = frame[:, None] * frequency[None, :]
    cosine = np.zeros((ROWS, 128), np.float32)
    sine = np.zeros((ROWS, 128), np.float32)
    cosine[:, :half] = cosine[:, half:HEAD] = np.cos(angle)
    sine[:, :half] = -np.sin(angle)
    sine[:, half:HEAD] = np.sin(angle)
    return cosine, sine


def modded_kernel(latents_in, modulation_in, modded_out, latents, modulation, modded, sems):
    start = copier(sems)
    arrivals = [start(latents_in, latents), start(modulation_in, modulation)]
    for copy in arrivals:
        copy.wait()
    normed, _ = normalise(latents[...].astype(F32))
    modded[...] = (normed * (1.0 + modulation[1, 0:1]) + modulation[0, 0:1]).astype(BF16)
    start(modded, modded_out).wait()


def modded_rows(*operands):
    out = jax.ShapeDtypeStruct((ROWS, WIDTH), BF16)
    return call(
        modded_kernel,
        out,
        [like(v) for v in operands] + [like(out), pltpu.SemaphoreType.DMA((3,))],
        [HBM] * 2,
        limit=60,
        out_space=pltpu.HBM,
    )(*operands)


def prologue_kernel(place, *refs):
    sources, outs, held = refs[:2], refs[2:4], refs[4:6]
    part, first_part, rest, sems = refs[6:]
    start = copier(sems)
    arrivals = [start(a, b) for a, b in zip(sources, held)]
    qkv, out = held
    rest[...] = jnp.zeros_like(rest)
    for copy in arrivals:
        copy.wait()
    for head in range(HEADS):

        @pl.when(place[0] == head)
        def _():
            for k in range(3):
                begin = k * FEATURES + head * HEAD
                both = qkv[:, :, begin : begin + HEAD].astype(F32)
                rest[0, :, k * HEAD : k * HEAD + HEAD] = both[:, 0]
                rest[1, :, k * HEAD : k * HEAD + HEAD] = both[:, 1]
            main = out[:, :, 128 * head : 128 * head + 128].astype(F32)
            tail = out[:, :, 1024 + 16 * head : 1040 + 16 * head].astype(F32)
            for block in range(2):
                rows = slice(18 * block, 18 * block + 18)
                rest[1, rows, 216:232] = tail[:, block]
                rest[1, rows, 256:384] = main[:, block]

    first = jnp.concatenate([rest[0, :, :128], rest[0, :, 128:256]], 0).astype(BF16)
    tiles = jnp.concatenate([rest[1, :, 128 * t : 128 * t + 128] for t in range(3)], 0)
    mine = jnp.where(place[1] == 0, tiles[:54], tiles[54:])
    mine = jnp.concatenate([mine, jnp.zeros((2, 128), F32)], 0).astype(BF16)
    for copy in range(32):
        part[copy] = mine
        first_part[copy] = first
    finish = [start(part, outs[0]), start(first_part, outs[1])]
    for copy in finish:
        copy.wait()


def prologue(place, *operands):
    outs = (
        jax.ShapeDtypeStruct((32, 56, 128), BF16),
        jax.ShapeDtypeStruct((32, 72, 128), BF16),
    )
    return call(
        prologue_kernel,
        outs,
        [like(v) for v in operands]
        + [like(v) for v in outs]
        + [pltpu.VMEM((2, 36, 384), F32), pltpu.SemaphoreType.DMA((4,))],
        [SMEM] + [HBM] * 2,
        limit=60,
        out_space=pltpu.HBM,
    )(place, *operands)


def adapters_kernel(place, down, up, down_first, down_second, up_first, up_second, held):
    for block in range(2):
        high, low = halves(down[block])
        down_parts = down_second if block else down_first
        down_parts[:64] = high
        down_parts[64:] = low
        for head in range(HEADS):
            start = head * HEAD
            columns = [up[block, :, k * FEATURES + start : k * FEATURES + start + HEAD] for k in range(3)]
            zero = jnp.zeros((RANK, 128 - HEAD), F32)
            wide = join_heads(*[jnp.concatenate([part, zero], 1) for part in columns])
            high, low = halves(wide)
            parts = jnp.concatenate([high, low, high], 0)
            if block == 0:
                held[head] = parts
            else:
                up_second[head] = parts
    up_first[...] = held[place[0]]


def adapters(place, down, up):
    return call(
        adapters_kernel,
        (
            jax.ShapeDtypeStruct((128, WIDTH), BF16),
            jax.ShapeDtypeStruct((128, WIDTH), BF16),
            jax.ShapeDtypeStruct((192, 256), BF16),
            jax.ShapeDtypeStruct((HEADS, 192, 256), BF16),
        ),
        [pltpu.VMEM((HEADS, 192, 256), BF16)],
        [SMEM, VMEM, VMEM],
    )(place, down, up)


def spatial_kernel(
    modded,
    weight,
    down,
    up,
    latents,
    targets,
    sent,
    projected,
    reduced,
    weights,
    merged,
):
    for chunk in range(32):
        rows = slice(36 * chunk, 36 * chunk + 36)
        merged[rows, :128] = weight[chunk, :36]
        merged[rows, 128:] = weight[chunk, 36:]
    sent[:, :, 640 : 640 + WIDTH] = latents[...].astype(F32).reshape(16, 8, WIDTH).astype(BF16)
    sent[:, :, 640 + WIDTH :] = targets[...].astype(F32).reshape(16, 8, WIDTH).astype(BF16)
    sent[:, :, FEATURES:640] = jnp.zeros((16, 8, 640 - FEATURES), BF16)
    rows = modded[...].reshape(8 * ROWS, WIDTH)
    low = dot(rows, down[...], NT)
    high, rest = halves(low[:, :64] + low[:, 64:])
    reduced[...] = jnp.concatenate([high, rest], 1)
    adapted = dot(jnp.concatenate([high, high, rest], 1), up[...])
    projected[...] = dot(rows, merged[...]) + adapted
    for frame in range(8):
        q, k, v = split_heads(projected[frame * ROWS : frame * ROWS + ROWS])
        q = (q * head_rate(q)).astype(BF16)
        k = (k * head_rate(k)).astype(BF16)
        w = softmax(dot(q, k, NT), None)
        weights[frame] = w
        attended = dot(w.astype(BF16), v.astype(BF16)).reshape(16, 8, 128)
        sent[:, :, HEAD * frame : HEAD * frame + HEAD] = attended[:, :, :HEAD].astype(BF16)


def spatial(*operands):
    return call(
        spatial_kernel,
        (
            jax.ShapeDtypeStruct((16, 8, 640 + 2 * WIDTH), BF16),
            jax.ShapeDtypeStruct((8 * ROWS, 256), F32),
            jax.ShapeDtypeStruct((8 * ROWS, 128), BF16),
            jax.ShapeDtypeStruct((8, ROWS, ROWS), F32),
        ),
        [pltpu.VMEM((WIDTH, 256), BF16)],
        us=8,
    )(*operands)


def spatial_back_kernel(
    cotangent, up, modded, projected, reduced, weights, grad, d_projected
):
    for pair in range(4):
        rows = cotangent[:, 16 * pair : 16 * pair + 16, :].astype(F32).reshape(16, 2, 8, 128)
        for side in range(2):
            frame = 2 * pair + side
            span = slice(frame * ROWS, frame * ROWS + ROWS)
            q, k, v = split_heads(projected[span])
            q_out = (q * head_rate(q)).astype(BF16)
            k_out = (k * head_rate(k)).astype(BF16)
            d_q, d_k, d_v = attention_back(
                weights[frame],
                q_out,
                k_out,
                v.astype(BF16),
                rows[:, side].reshape(ROWS, 128).astype(BF16),
            )
            d_projected[span] = join_heads(head_norm_back(q, d_q), head_norm_back(k, d_k), d_v)
    high, rest = halves(d_projected[...])
    both = dot(reduced[...], jnp.concatenate([high, rest], 1), TN)
    grad_up = both[:64, :256] + both[64:, :256] + both[:64, 256:] + both[64:, 256:]
    head = up[:128]
    two = dot(high, head, NT) + dot(rest, head, NT)
    low_high, low_rest = halves(two[:, :64] + two[:, 64:])
    down = dot(
        jnp.concatenate([low_high, low_rest], 1), modded[...].reshape(8 * ROWS, WIDTH), TN
    )
    store_tiles(grad, 0, down[:64] + down[64:])
    store_tiles(grad, 9, grad_up)


def store_tiles(ref, start, values):
    for tile in range(values.shape[1] // 128):
        ref[:, start + tile, :] = values[:, 128 * tile : 128 * tile + 128]


def spatial_back(*operands):
    return call(
        spatial_back_kernel,
        jax.ShapeDtypeStruct((RANK, 11, 128), F32),
        [pltpu.VMEM((8 * ROWS, 256), F32)],
        us=20,
    )(*operands)


def part_copies(gathered, held, start):
    return [start(gathered.at[pl.ds(4 * x, 4)], held.at[pl.ds(4 * x, 4)]) for x in range(4)]


def assemble(copies, held, qkv, out_first, out_second):
    for x in range(4):
        copies[x].wait()
        for c in range(2):
            head = 2 * x + c
            lower, upper = held.at[4 * x + c], held.at[4 * x + 2 + c]
            main = slice(128 * head, 128 * head + 128)
            tail = slice(1024 + 16 * head, 1040 + 16 * head)
            for d in range(32):
                a = 36 * d
                qkv[head, a : a + 36, :128] = lower[d, 0:36]
                qkv[head, a : a + 18, 128:] = lower[d, 36:54]
                qkv[head, a + 18 : a + 36, 128:] = upper[d, 0:18]
                rows = slice(18 * d, 18 * d + 18)
                out_first[rows, main] = upper[d, 18:36]
                out_second[rows, main] = upper[d, 36:54]
                out_first[rows, tail] = lower[d, 36:54, 88:104]
                out_second[rows, tail] = upper[d, 0:18, 88:104]


def by_rows(received, columns):
    values = received[:, :, columns].astype(F32)
    frames = [x * 4 + l * 2 + c for l in range(2) for x in range(4) for c in range(2)]
    return jnp.concatenate([values[f] for f in frames], 0)


def temporal_kernel(
    gathered,
    received_in,
    modulation_in,
    down_in,
    up_in,
    cosine_in,
    sine_in,
    sent_out,
    grad_out,
    received,
    modulation,
    down,
    up,
    cosine,
    sine,
    sent,
    grad,
    wide,
    modded,
    reduced,
    d_projected,
    ups,
    projected,
    weights,
    q_all,
    k_all,
    v_all,
    held,
    qkv,
    out_first,
    out_second,
    d_out,
    d_v,
    d_weights,
    d_scores,
    d_q,
    d_k,
    sems,
):
    start = copier(sems)
    received_copy = start(received_in, received)
    copies = part_copies(gathered, held, start)
    arrivals = [
        start(modulation_in, modulation),
        start(down_in, down),
        start(up_in, up),
        start(cosine_in, cosine),
        start(sine_in, sine),
    ]
    received_copy.wait()
    for head in range(HEADS):
        x, c = head // 2, head % 2
        rows = jnp.concatenate(
            [
                received[x * 4 + 2 * l + c, :, HEAD * g : HEAD * g + HEAD].astype(F32)
                for l in range(2)
                for g in range(8)
            ],
            0,
        )
        wide[:, HEAD * head : HEAD * head + HEAD] = rows
    assemble(copies, held, qkv, out_first, out_second)
    for copy in arrivals:
        copy.wait()
    gate_first, gate_second = modulation[2, 0:1], modulation[2, 1:2]
    mixed = dot(wide[...].astype(BF16), out_first[...])
    middle = (by_rows(received, slice(640, 640 + WIDTH)) + gate_first * mixed).astype(BF16).astype(F32)
    normed, rate = normalise(middle)
    scale = 1.0 + modulation[1, 1:2]
    modded[...] = (normed * scale + modulation[0, 1:2]).astype(BF16)
    low = dot(modded[...], down[...], NT)
    high, rest = halves(low[:, :64] + low[:, 64:])
    reduced[...] = jnp.concatenate([high, rest], 1)
    three = jnp.concatenate([high, high, rest], 1)
    mask = same_token()
    for head in range(HEADS):
        projected[head] = dot(modded[...], qkv[head]) + dot(three, up[head])
    q, k, v = split_heads(projected[...].reshape(HEADS * ROWS, 256))
    q = (q * head_rate(q)).reshape(HEADS, ROWS, 128)
    k = (k * head_rate(k)).reshape(HEADS, ROWS, 128)
    q_all[...] = (q * cosine[...] + swap(q) * sine[...]).astype(BF16)
    k_all[...] = (k * cosine[...] + swap(k) * sine[...]).astype(BF16)
    v_all[...] = v.astype(BF16).reshape(HEADS, ROWS, 128)
    for head in range(HEADS):
        weights[head] = dot(q_all[head], k_all[head], NT)
    weights[...] = softmax(weights[...], mask)
    for head in range(HEADS):
        wide[:, HEAD * head : HEAD * head + HEAD] = dot(weights[head].astype(BF16), v_all[head])[:, :HEAD]
    mixed = dot(wide[...].astype(BF16), out_second[...])
    produced = (middle + gate_second * mixed).astype(BF16).astype(F32)
    error = ((produced - by_rows(received, slice(640 + WIDTH, None))) / WIDTH).astype(BF16).astype(F32)
    wide[...] = dot((gate_second * error).astype(BF16), out_second[...], NT)
    for head in range(HEADS):
        cotangent = wide[:, HEAD * head : HEAD * head + HEAD].astype(BF16)
        d_out[head] = jnp.concatenate([cotangent, jnp.zeros((ROWS, 128 - HEAD), BF16)], 1)
    for head in range(HEADS):
        d_v[head] = dot(weights[head].astype(BF16), d_out[head], TN)
        d_weights[head] = dot(d_out[head], v_all[head], NT)
    inner = d_weights[...].astype(BF16).astype(F32)
    inner = weights[...] * (inner - jnp.sum(inner * weights[...], -1, keepdims=True))
    d_scores[...] = (inner * SCALE).astype(BF16)
    for head in range(HEADS):
        d_q[head] = dot(d_scores[head], k_all[head])
        d_k[head] = dot(d_scores[head], q_all[head], TN)
    back = []
    q, k, _ = split_heads(projected[...].reshape(HEADS * ROWS, 256))
    for values, ref in ((q, d_q), (k, d_k)):
        d = ref[...].astype(BF16).astype(F32)
        d = (d * cosine[...] - swap(d) * sine[...]).reshape(HEADS * ROWS, 128)
        back.append(head_norm_back(values, d))
    d_val = d_v[...].astype(BF16).astype(F32).reshape(HEADS * ROWS, 128)
    d_projected[...] = join_heads(*back, d_val).reshape(HEADS, ROWS, 256)
    d_low = jnp.zeros((ROWS, 128), F32)
    d_modded = jnp.zeros((ROWS, WIDTH), F32)
    for head in range(HEADS):
        high, rest = halves(d_projected[head])
        d_low += dot(high, up[head, :128], NT) + dot(rest, up[head, :128], NT)
        d_modded += dot(high, qkv[head], NT)
    d_low = d_low[:, :64] + d_low[:, 64:]
    high, rest = halves(d_low)
    d_reduced = jnp.concatenate([high, rest], 1)
    through = dot(jnp.concatenate([high, high], 1), down[...]) + dot(rest, down[:64])
    d_modded = (d_modded.astype(BF16) + through.astype(BF16)).astype(F32)
    d_normed = d_modded * scale
    inner = jnp.mean(d_normed * normed, -1, keepdims=True)
    d_middle = rate * (d_normed - jnp.mean(d_normed, -1, keepdims=True) - normed * inner)
    d_middle = (error.astype(BF16) + d_middle.astype(BF16)).astype(F32)
    wide[...] = dot((gate_first * d_middle).astype(BF16), out_first[...], NT)
    for head in range(HEADS):
        x, c = head // 2, head % 2
        rows = wide[:, HEAD * head : HEAD * head + HEAD].astype(BF16)
        rows = jnp.concatenate([rows, jnp.zeros((ROWS, 128 - HEAD), BF16)], 1)
        sent[x * 4 + c] = rows[:64]
        sent[x * 4 + 2 + c] = rows[64:]
    sent_copy = start(sent, sent_out)
    ups[:, 1664:] = jnp.zeros((64, 128), F32)
    for head in range(HEADS):
        high, rest = halves(d_projected[head])
        both = dot(reduced[...], jnp.concatenate([high, rest], 1), TN)
        part = both[:64, :256] + both[64:, :256] + both[:64, 256:] + both[64:, 256:]
        for k in range(3):
            begin = k * FEATURES + head * HEAD
            ups[:, begin : begin + HEAD] = part[:, k * HEAD : k * HEAD + HEAD]
    down = dot(d_reduced, modded[...], TN)
    store_tiles(grad, 0, down[:64] + down[64:])
    store_tiles(grad, 9, ups[...])
    start(grad, grad_out).wait()
    sent_copy.wait()


def temporal(gathered, *operands):
    return call(
        temporal_kernel,
        (
            jax.ShapeDtypeStruct((16, 64, 128), BF16),
            jax.ShapeDtypeStruct((RANK, 23, 128), F32),
        ),
        [like(v) for v in operands]
        + [
            pltpu.VMEM((16, 64, 128), BF16),
            pltpu.VMEM((RANK, 23, 128), F32),
            pltpu.VMEM((ROWS, FEATURES), F32),
            pltpu.VMEM((ROWS, WIDTH), BF16),
            pltpu.VMEM((ROWS, 128), BF16),
            pltpu.VMEM((HEADS, ROWS, 256), F32),
            pltpu.VMEM((RANK, 1792), F32),
            pltpu.VMEM((HEADS, ROWS, 256), F32),
            pltpu.VMEM((HEADS, ROWS, ROWS), F32),
            pltpu.VMEM((HEADS, ROWS, 128), BF16),
            pltpu.VMEM((HEADS, ROWS, 128), BF16),
            pltpu.VMEM((HEADS, ROWS, 128), BF16),
            pltpu.VMEM((16, 32, 56, 128), BF16),
            pltpu.VMEM((HEADS, WIDTH, 256), BF16),
            pltpu.VMEM((FEATURES, WIDTH), BF16),
            pltpu.VMEM((FEATURES, WIDTH), BF16),
            pltpu.VMEM((HEADS, ROWS, 128), BF16),
            pltpu.VMEM((HEADS, ROWS, 128), F32),
            pltpu.VMEM((HEADS, ROWS, ROWS), F32),
            pltpu.VMEM((HEADS, ROWS, ROWS), BF16),
            pltpu.VMEM((HEADS, ROWS, 128), F32),
            pltpu.VMEM((HEADS, ROWS, 128), F32),
            pltpu.SemaphoreType.DMA((12,)),
        ],
        [HBM] * 7,
        limit=60,
        out_space=pltpu.HBM,
        us=25,
    )(gathered, *operands)


def epilogue_kernel(place, own, other, grad_down, grad_up):
    for side, ref in enumerate((own, other)):
        core = place[2] if side == 0 else 1 - place[2]
        rows = pl.ds(pl.multiple_of(core * 32, 32), 32)
        for tile in range(9):
            columns = slice(128 * tile, 128 * tile + 128)
            grad_down[0, rows, columns] = ref[:, tile, :]
            grad_down[1, rows, columns] = ref[:, 25 + tile, :]
        for head in range(HEADS):
            both = jnp.concatenate([ref[:, 9 + 2 * head, :], ref[:, 10 + 2 * head, :]], 1)
            for k in range(3):
                start = k * FEATURES + head * HEAD
                grad_up[0, rows, start : start + HEAD] = both[:, k * HEAD : k * HEAD + HEAD]
        for tile in range(13):
            grad_up[1, rows, 128 * tile : 128 * tile + 128] = ref[:, 34 + tile, :]
        grad_up[1, rows, 1664:1728] = ref[:, 47, :][:, :64]


def epilogue(place, own, other):
    vmem = spec(pltpu.VMEM)
    return call(
        epilogue_kernel,
        (
            jax.ShapeDtypeStruct((2, RANK, WIDTH), F32),
            jax.ShapeDtypeStruct((2, RANK, 3 * FEATURES), F32),
        ),
        in_specs=[spec(pltpu.SMEM), vmem, vmem],
    )(place, own, other)


def exchange(values, axes):
    return lax.all_to_all(values, axes, 0, 0)


def spread(values, axes, count):
    return exchange(jnp.broadcast_to(values[None], (count,) + values.shape), axes)


def swap_cores(values):
    return lax.ppermute(values, "c", [(0, 1), (1, 0)])


def add_cores(values, c):
    mine = lax.dynamic_slice_in_dim(values, c * 32, 32, 0)
    return mine, swap_cores(lax.dynamic_slice_in_dim(values, (1 - c) * 32, 32, 0))


def on_device(latents, targets, modulation, qkv, out, down, up):
    x, l, c = lax.axis_index("x"), lax.axis_index("l"), lax.axis_index("c")
    place = jnp.stack([x * 2 + c, l, c]).astype(jnp.int32)
    modulation = modulation[0].transpose(1, 0, 2)
    modded = modded_rows(latents[0, 0], modulation)
    part, first = prologue(place, qkv.transpose(1, 0, 2), out.transpose(1, 0, 2))
    modded = lax.all_gather(modded, ("x", "c"), axis=0, tiled=False)
    gathered = lax.all_gather(exchange(part, DP), SEQ, axis=0, tiled=False)
    first = exchange(first, DP)
    down_first, down_second, up_first, up_second = adapters(place, down.transpose(0, 2, 1), up)
    sent, projected, reduced, weights = spatial(
        modded, first, down_first, up_first, latents[0, 0], targets[0, 0]
    )
    received = exchange(sent, SEQ)
    cosine, sine = rotation_tables()
    sent, late = temporal(
        gathered,
        received,
        modulation,
        down_second,
        up_second,
        jnp.asarray(cosine),
        jnp.asarray(sine),
    )
    cotangent = exchange(sent, SEQ)
    late = sum(add_cores(late, c))
    early = spatial_back(cotangent, up_first, modded, projected, reduced, weights)
    mine, other = add_cores(early, c)
    first_up, second_up = mine[:, 9:], other[:, 9:]
    total = jnp.concatenate(
        [
            mine[:, :9] + other[:, :9],
            jnp.where(c == 0, first_up, second_up),
            jnp.where(c == 0, second_up, first_up),
            late,
        ],
        1,
    )
    total = exchange(total.reshape(32, 9, 4, 128), ("z", "x")).reshape(32, 36, 128)
    ups = jnp.sum(total[:, 9:13].reshape(8, 4, 4, 128), 0).reshape(16, 128)
    total = jnp.concatenate([jnp.sum(total[:, :9], 0), ups, jnp.sum(total[:, 13:], 0)], 0)
    total = jnp.sum(spread(total, ("h", "l"), 8), 0)
    total = spread(total, ("z", "x"), 32)
    grad_down, grad_up = epilogue(place, total, swap_cores(total))
    return grad_down.transpose(0, 2, 1), grad_up


def solution(mesh):
    inner = Mesh(mesh.devices.reshape(8, 4, 4, 2, 2), ("z", "h", "x", "l", "c"))
    in_specs = (
        P(DP, SEQ, None, None),
        P(DP, SEQ, None, None),
        P(DP, None, None, None),
        P(None, DP, None),
        P(None, DP, None),
        P(),
        P(),
    )
    return jax.shard_map(
        on_device, mesh=inner, in_specs=in_specs, out_specs=(P(), P()), check_vma=False
    )
```

```python
import math

import jax
import jax.numpy as jnp
import numpy as np
from jax import lax
from jax.experimental import pallas as pl
from jax.experimental.pallas import tpu as pltpu
from jax.sharding import Mesh, PartitionSpec as P

WIDTH = 1152
HEADS = 8
HEAD = 72
RANK = 64
FEATURES = HEADS * HEAD
ROWS = 128
F32 = jnp.float32
BF16 = jnp.bfloat16
SCALE = 1.0 / math.sqrt(HEAD)
MIB = 1 << 20
DP = ("z", "h")
SEQ = ("x", "l", "c")


def call(kernel, out_shape, scratch=(), in_specs=None, limit=20, out_space=pltpu.VMEM, us=2):
    vmem = pl.BlockSpec(memory_space=pltpu.VMEM)
    out_spec = pl.BlockSpec(memory_space=out_space)

    def run(*operands):
        return pl.pallas_call(
            kernel,
            out_shape=out_shape,
            in_specs=in_specs or [vmem] * len(operands),
            out_specs=jax.tree.map(lambda _: out_spec, out_shape),
            scratch_shapes=list(scratch),
            compiler_params=pltpu.CompilerParams(vmem_limit_bytes=limit * MIB),
            cost_estimate=pl.CostEstimate(
                flops=us * 10**9, bytes_accessed=us * 3 * 10**6, transcendentals=0
            ),
        )(*operands)

    return run


def spec(space):
    return pl.BlockSpec(memory_space=space)


SMEM, VMEM, HBM = spec(pltpu.SMEM), spec(pltpu.VMEM), spec(pltpu.HBM)


def copier(sems):
    count = iter(range(100))

    def start(source, target):
        copy = pltpu.make_async_copy(source, target, sems.at[next(count)])
        copy.start()
        return copy

    return start


def like(values):
    return pltpu.VMEM(values.shape, values.dtype)


def dot(a, b, dims=((1,), (0,))):
    return lax.dot_general(a, b, (dims, ((), ())), preferred_element_type=F32)


NT = ((1,), (1,))
TN = ((0,), (0,))


def halves(values):
    high = values.astype(BF16)
    return high, (values - high.astype(F32)).astype(BF16)


def normalise(values):
    centred = values - jnp.mean(values, -1, keepdims=True)
    rate = lax.rsqrt(jnp.mean(centred * centred, -1, keepdims=True) + 1e-06)
    return centred * rate, rate


def lane_mask(width, dtype=F32):
    lanes = lax.broadcasted_iota(jnp.int32, (1, 128), 1)
    return (lanes < width).astype(dtype)


def split_heads(projected):
    keep = lane_mask(HEAD)
    q = projected[:, :128] * keep
    k = pltpu.roll(projected, 256 - HEAD, 1)[:, :128] * keep
    v = pltpu.roll(projected, 256 - 2 * HEAD, 1)[:, :128] * keep
    return q, k, v


def join_heads(q, k, v):
    zero = jnp.zeros_like(q)
    return (
        jnp.concatenate([q, zero], 1)
        + pltpu.roll(jnp.concatenate([k, zero], 1), HEAD, 1)
        + pltpu.roll(jnp.concatenate([v, zero], 1), 2 * HEAD, 1)
    )


def head_rate(values):
    return lax.rsqrt(jnp.sum(values * values, -1, keepdims=True) * (1.0 / HEAD) + 1e-06)


def head_norm_back(values, cotangent):
    rate = head_rate(values)
    inner = jnp.sum(cotangent * values, -1, keepdims=True) * (1.0 / HEAD)
    return rate * (cotangent - values * (rate * rate * inner))


def swap(values):
    lanes = lax.broadcasted_iota(jnp.int32, (1, 128), 1)
    return jnp.where(
        lanes < HEAD // 2,
        pltpu.roll(values, 128 - HEAD // 2, values.ndim - 1),
        pltpu.roll(values, HEAD // 2, values.ndim - 1),
    )


def softmax(scores, mask):
    weights = jnp.exp(scores * SCALE)
    if mask is not None:
        weights = weights * mask
    return weights / jnp.sum(weights, -1, keepdims=True)


def attention_back(weights, q, k, v, cotangent):
    rounded = weights.astype(BF16)
    d_v = dot(rounded, cotangent, TN).astype(BF16)
    d_weights = dot(cotangent, v, NT).astype(BF16).astype(F32)
    d_scores = weights * (d_weights - jnp.sum(d_weights * weights, -1, keepdims=True))
    d_scores = (d_scores * SCALE).astype(BF16)
    d_q = dot(d_scores, k).astype(BF16)
    d_k = dot(d_scores, q, TN).astype(BF16)
    return d_q.astype(F32), d_k.astype(F32), d_v.astype(F32)


def same_token():
    rows = lax.broadcasted_iota(jnp.int32, (ROWS, ROWS), 0)
    columns = lax.broadcasted_iota(jnp.int32, (ROWS, ROWS), 1)
    return ((rows & 7) == (columns & 7)).astype(F32)


def rotation_tables():
    row = np.arange(ROWS)
    frame = ((row // 16) % 4) * 4 + (row // 64) * 2 + (row // 8) % 2
    half = HEAD // 2
    frequency = np.exp(np.arange(half) * (-2.0 * math.log(10000.0) / HEAD))
    angle = frame[:, None] * frequency[None, :]
    cosine = np.zeros((ROWS, 128), np.float32)
    sine = np.zeros((ROWS, 128), np.float32)
    cosine[:, :half] = cosine[:, half:HEAD] = np.cos(angle)
    sine[:, :half] = -np.sin(angle)
    sine[:, half:HEAD] = np.sin(angle)
    return cosine, sine


def prologue_kernel(place, *refs):
    sources, outs, held = refs[:4], refs[4:7], refs[7:11]
    modded, part, first_part, rest, sems = refs[11:]
    start = copier(sems)
    arrivals = [start(a, b) for a, b in zip(sources, held)]
    latents, modulation, qkv, out = held
    arrivals[0].wait()
    arrivals[1].wait()
    normed, _ = normalise(latents[...].astype(F32))
    modded[...] = (normed * (1.0 + modulation[1, 0:1]) + modulation[0, 0:1]).astype(BF16)
    finish = [start(modded, outs[0])]
    rest[...] = jnp.zeros_like(rest)
    arrivals[2].wait()
    arrivals[3].wait()
    for head in range(HEADS):

        @pl.when(place[0] == head)
        def _():
            for k in range(3):
                begin = k * FEATURES + head * HEAD
                both = qkv[:, :, begin : begin + HEAD].astype(F32)
                rest[0, :, k * HEAD : k * HEAD + HEAD] = both[:, 0]
                rest[1, :, k * HEAD : k * HEAD + HEAD] = both[:, 1]
            main = out[:, :, 128 * head : 128 * head + 128].astype(F32)
            tail = out[:, :, 1024 + 16 * head : 1040 + 16 * head].astype(F32)
            for block in range(2):
                rows = slice(18 * block, 18 * block + 18)
                rest[1, rows, 216:232] = tail[:, block]
                rest[1, rows, 256:384] = main[:, block]

    first = jnp.concatenate([rest[0, :, :128], rest[0, :, 128:256]], 0).astype(BF16)
    tiles = jnp.concatenate([rest[1, :, 128 * t : 128 * t + 128] for t in range(3)], 0)
    mine = jnp.where(place[1] == 0, tiles[:54], tiles[54:])
    mine = jnp.concatenate([mine, jnp.zeros((2, 128), F32)], 0).astype(BF16)
    for copy in range(32):
        part[copy] = mine
        first_part[copy] = first
    finish += [start(part, outs[1]), start(first_part, outs[2])]
    for copy in finish:
        copy.wait()


def prologue(place, *operands):
    outs = (
        jax.ShapeDtypeStruct((ROWS, WIDTH), BF16),
        jax.ShapeDtypeStruct((32, 56, 128), BF16),
        jax.ShapeDtypeStruct((32, 72, 128), BF16),
    )
    return call(
        prologue_kernel,
        outs,
        [like(v) for v in operands]
        + [like(v) for v in outs]
        + [pltpu.VMEM((2, 36, 384), F32), pltpu.SemaphoreType.DMA((7,))],
        [SMEM] + [HBM] * 4,
        limit=60,
        out_space=pltpu.HBM,
    )(place, *operands)


def adapters_kernel(place, down, up, down_first, down_second, up_first, up_second, held):
    for block in range(2):
        high, low = halves(down[block])
        down_parts = down_second if block else down_first
        down_parts[:64] = high
        down_parts[64:] = low
        for head in range(HEADS):
            start = head * HEAD
            columns = [up[block, :, k * FEATURES + start : k * FEATURES + start + HEAD] for k in range(3)]
            zero = jnp.zeros((RANK, 128 - HEAD), F32)
            wide = join_heads(*[jnp.concatenate([part, zero], 1) for part in columns])
            high, low = halves(wide)
            parts = jnp.concatenate([high, low, high], 0)
            if block == 0:
                held[head] = parts
            else:
                up_second[head] = parts
    up_first[...] = held[place[0]]


def adapters(place, down, up):
    return call(
        adapters_kernel,
        (
            jax.ShapeDtypeStruct((128, WIDTH), BF16),
            jax.ShapeDtypeStruct((128, WIDTH), BF16),
            jax.ShapeDtypeStruct((192, 256), BF16),
            jax.ShapeDtypeStruct((HEADS, 192, 256), BF16),
        ),
        [pltpu.VMEM((HEADS, 192, 256), BF16)],
        [SMEM, VMEM, VMEM],
    )(place, down, up)


def spatial_kernel(
    modded,
    weight,
    down,
    up,
    latents,
    targets,
    sent,
    projected,
    reduced,
    weights,
    merged,
):
    for chunk in range(32):
        rows = slice(36 * chunk, 36 * chunk + 36)
        merged[rows, :128] = weight[chunk, :36]
        merged[rows, 128:] = weight[chunk, 36:]
    sent[:, :, 640 : 640 + WIDTH] = latents[...].astype(F32).reshape(16, 8, WIDTH).astype(BF16)
    sent[:, :, 640 + WIDTH :] = targets[...].astype(F32).reshape(16, 8, WIDTH).astype(BF16)
    sent[:, :, FEATURES:640] = jnp.zeros((16, 8, 640 - FEATURES), BF16)
    rows = modded[...].reshape(8 * ROWS, WIDTH)
    low = dot(rows, down[...], NT)
    high, rest = halves(low[:, :64] + low[:, 64:])
    reduced[...] = jnp.concatenate([high, rest], 1)
    adapted = dot(jnp.concatenate([high, high, rest], 1), up[...])
    projected[...] = dot(rows, merged[...]) + adapted
    for frame in range(8):
        q, k, v = split_heads(projected[frame * ROWS : frame * ROWS + ROWS])
        q = (q * head_rate(q)).astype(BF16)
        k = (k * head_rate(k)).astype(BF16)
        w = softmax(dot(q, k, NT), None)
        weights[frame] = w
        attended = dot(w.astype(BF16), v.astype(BF16)).reshape(16, 8, 128)
        sent[:, :, HEAD * frame : HEAD * frame + HEAD] = attended[:, :, :HEAD].astype(BF16)


def spatial(*operands):
    return call(
        spatial_kernel,
        (
            jax.ShapeDtypeStruct((16, 8, 640 + 2 * WIDTH), BF16),
            jax.ShapeDtypeStruct((8 * ROWS, 256), F32),
            jax.ShapeDtypeStruct((8 * ROWS, 128), BF16),
            jax.ShapeDtypeStruct((8, ROWS, ROWS), F32),
        ),
        [pltpu.VMEM((WIDTH, 256), BF16)],
        us=8,
    )(*operands)


def spatial_back_kernel(
    cotangent, up, modded, projected, reduced, weights, grad, d_projected
):
    for pair in range(4):
        rows = cotangent[:, 16 * pair : 16 * pair + 16, :].astype(F32).reshape(16, 2, 8, 128)
        for side in range(2):
            frame = 2 * pair + side
            span = slice(frame * ROWS, frame * ROWS + ROWS)
            q, k, v = split_heads(projected[span])
            q_out = (q * head_rate(q)).astype(BF16)
            k_out = (k * head_rate(k)).astype(BF16)
            d_q, d_k, d_v = attention_back(
                weights[frame],
                q_out,
                k_out,
                v.astype(BF16),
                rows[:, side].reshape(ROWS, 128).astype(BF16),
            )
            d_projected[span] = join_heads(head_norm_back(q, d_q), head_norm_back(k, d_k), d_v)
    high, rest = halves(d_projected[...])
    both = dot(reduced[...], jnp.concatenate([high, rest], 1), TN)
    grad_up = both[:64, :256] + both[64:, :256] + both[:64, 256:] + both[64:, 256:]
    head = up[:128]
    two = dot(high, head, NT) + dot(rest, head, NT)
    low_high, low_rest = halves(two[:, :64] + two[:, 64:])
    down = dot(
        jnp.concatenate([low_high, low_rest], 1), modded[...].reshape(8 * ROWS, WIDTH), TN
    )
    store_tiles(grad, 0, down[:64] + down[64:])
    store_tiles(grad, 9, grad_up)


def store_tiles(ref, start, values):
    for tile in range(values.shape[1] // 128):
        ref[:, start + tile, :] = values[:, 128 * tile : 128 * tile + 128]


def spatial_back(*operands):
    return call(
        spatial_back_kernel,
        jax.ShapeDtypeStruct((RANK, 11, 128), F32),
        [pltpu.VMEM((8 * ROWS, 256), F32)],
        us=20,
    )(*operands)


def part_copies(gathered, held, start):
    return [start(gathered.at[pl.ds(4 * x, 4)], held.at[pl.ds(4 * x, 4)]) for x in range(4)]


def assemble(copies, held, qkv, out_first, out_second):
    for x in range(4):
        copies[x].wait()
        for c in range(2):
            head = 2 * x + c
            lower, upper = held.at[4 * x + c], held.at[4 * x + 2 + c]
            main = slice(128 * head, 128 * head + 128)
            tail = slice(1024 + 16 * head, 1040 + 16 * head)
            for d in range(32):
                a = 36 * d
                qkv[head, a : a + 36, :128] = lower[d, 0:36]
                qkv[head, a : a + 18, 128:] = lower[d, 36:54]
                qkv[head, a + 18 : a + 36, 128:] = upper[d, 0:18]
                rows = slice(18 * d, 18 * d + 18)
                out_first[rows, main] = upper[d, 18:36]
                out_second[rows, main] = upper[d, 36:54]
                out_first[rows, tail] = lower[d, 36:54, 88:104]
                out_second[rows, tail] = upper[d, 0:18, 88:104]


def by_rows(received, columns):
    values = received[:, :, columns].astype(F32)
    frames = [x * 4 + l * 2 + c for l in range(2) for x in range(4) for c in range(2)]
    return jnp.concatenate([values[f] for f in frames], 0)


def temporal_kernel(
    gathered,
    received_in,
    modulation_in,
    down_in,
    up_in,
    cosine_in,
    sine_in,
    sent_out,
    modded_out,
    reduced_out,
    d_projected_out,
    d_reduced_out,
    received,
    modulation,
    down,
    up,
    cosine,
    sine,
    sent,
    wide,
    modded,
    reduced,
    d_projected,
    d_reduced,
    projected,
    weights,
    q_all,
    k_all,
    v_all,
    held,
    qkv,
    out_first,
    out_second,
    d_out,
    d_v,
    d_weights,
    d_scores,
    d_q,
    d_k,
    sems,
):
    start = copier(sems)
    received_copy = start(received_in, received)
    copies = part_copies(gathered, held, start)
    arrivals = [
        start(modulation_in, modulation),
        start(down_in, down),
        start(up_in, up),
        start(cosine_in, cosine),
        start(sine_in, sine),
    ]
    received_copy.wait()
    for head in range(HEADS):
        x, c = head // 2, head % 2
        rows = jnp.concatenate(
            [
                received[x * 4 + 2 * l + c, :, HEAD * g : HEAD * g + HEAD].astype(F32)
                for l in range(2)
                for g in range(8)
            ],
            0,
        )
        wide[:, HEAD * head : HEAD * head + HEAD] = rows
    assemble(copies, held, qkv, out_first, out_second)
    for copy in arrivals:
        copy.wait()
    gate_first, gate_second = modulation[2, 0:1], modulation[2, 1:2]
    mixed = dot(wide[...].astype(BF16), out_first[...])
    middle = (by_rows(received, slice(640, 640 + WIDTH)) + gate_first * mixed).astype(BF16).astype(F32)
    normed, rate = normalise(middle)
    scale = 1.0 + modulation[1, 1:2]
    modded[...] = (normed * scale + modulation[0, 1:2]).astype(BF16)
    low = dot(modded[...], down[...], NT)
    high, rest = halves(low[:, :64] + low[:, 64:])
    reduced[...] = jnp.concatenate([high, rest], 1)
    saves = [start(modded, modded_out), start(reduced, reduced_out)]
    three = jnp.concatenate([high, high, rest], 1)
    mask = same_token()
    for head in range(HEADS):
        projected[head] = dot(modded[...], qkv[head]) + dot(three, up[head])
    q, k, v = split_heads(projected[...].reshape(HEADS * ROWS, 256))
    q = (q * head_rate(q)).reshape(HEADS, ROWS, 128)
    k = (k * head_rate(k)).reshape(HEADS, ROWS, 128)
    q_all[...] = (q * cosine[...] + swap(q) * sine[...]).astype(BF16)
    k_all[...] = (k * cosine[...] + swap(k) * sine[...]).astype(BF16)
    v_all[...] = v.astype(BF16).reshape(HEADS, ROWS, 128)
    for head in range(HEADS):
        weights[head] = dot(q_all[head], k_all[head], NT)
    weights[...] = softmax(weights[...], mask)
    for head in range(HEADS):
        wide[:, HEAD * head : HEAD * head + HEAD] = dot(weights[head].astype(BF16), v_all[head])[:, :HEAD]
    mixed = dot(wide[...].astype(BF16), out_second[...])
    produced = (middle + gate_second * mixed).astype(BF16).astype(F32)
    error = ((produced - by_rows(received, slice(640 + WIDTH, None))) / WIDTH).astype(BF16).astype(F32)
    wide[...] = dot((gate_second * error).astype(BF16), out_second[...], NT)
    for head in range(HEADS):
        cotangent = wide[:, HEAD * head : HEAD * head + HEAD].astype(BF16)
        d_out[head] = jnp.concatenate([cotangent, jnp.zeros((ROWS, 128 - HEAD), BF16)], 1)
    for head in range(HEADS):
        d_v[head] = dot(weights[head].astype(BF16), d_out[head], TN)
        d_weights[head] = dot(d_out[head], v_all[head], NT)
    inner = d_weights[...].astype(BF16).astype(F32)
    inner = weights[...] * (inner - jnp.sum(inner * weights[...], -1, keepdims=True))
    d_scores[...] = (inner * SCALE).astype(BF16)
    for head in range(HEADS):
        d_q[head] = dot(d_scores[head], k_all[head])
        d_k[head] = dot(d_scores[head], q_all[head], TN)
    back = []
    q, k, _ = split_heads(projected[...].reshape(HEADS * ROWS, 256))
    for values, ref in ((q, d_q), (k, d_k)):
        d = ref[...].astype(BF16).astype(F32)
        d = (d * cosine[...] - swap(d) * sine[...]).reshape(HEADS * ROWS, 128)
        back.append(head_norm_back(values, d))
    d_val = d_v[...].astype(BF16).astype(F32).reshape(HEADS * ROWS, 128)
    d_projected[...] = join_heads(*back, d_val).reshape(HEADS, ROWS, 256)
    saves.append(start(d_projected, d_projected_out))
    d_low = jnp.zeros((ROWS, 128), F32)
    d_modded = jnp.zeros((ROWS, WIDTH), F32)
    for head in range(HEADS):
        high, rest = halves(d_projected[head])
        d_low += dot(high, up[head, :128], NT) + dot(rest, up[head, :128], NT)
        d_modded += dot(high, qkv[head], NT)
    d_low = d_low[:, :64] + d_low[:, 64:]
    high, rest = halves(d_low)
    d_reduced[...] = jnp.concatenate([high, rest], 1)
    saves.append(start(d_reduced, d_reduced_out))
    through = dot(jnp.concatenate([high, high], 1), down[...]) + dot(rest, down[:64])
    d_modded = (d_modded.astype(BF16) + through.astype(BF16)).astype(F32)
    d_normed = d_modded * scale
    inner = jnp.mean(d_normed * normed, -1, keepdims=True)
    d_middle = rate * (d_normed - jnp.mean(d_normed, -1, keepdims=True) - normed * inner)
    d_middle = (error.astype(BF16) + d_middle.astype(BF16)).astype(F32)
    wide[...] = dot((gate_first * d_middle).astype(BF16), out_first[...], NT)
    for head in range(HEADS):
        x, c = head // 2, head % 2
        rows = wide[:, HEAD * head : HEAD * head + HEAD].astype(BF16)
        rows = jnp.concatenate([rows, jnp.zeros((ROWS, 128 - HEAD), BF16)], 1)
        sent[x * 4 + c] = rows[:64]
        sent[x * 4 + 2 + c] = rows[64:]
    saves.append(start(sent, sent_out))
    for copy in saves:
        copy.wait()


def temporal(gathered, *operands):
    return call(
        temporal_kernel,
        (
            jax.ShapeDtypeStruct((16, 64, 128), BF16),
            jax.ShapeDtypeStruct((ROWS, WIDTH), BF16),
            jax.ShapeDtypeStruct((ROWS, 128), BF16),
            jax.ShapeDtypeStruct((HEADS, ROWS, 256), F32),
            jax.ShapeDtypeStruct((ROWS, 128), BF16),
        ),
        [like(v) for v in operands]
        + [
            pltpu.VMEM((16, 64, 128), BF16),
            pltpu.VMEM((ROWS, FEATURES), F32),
            pltpu.VMEM((ROWS, WIDTH), BF16),
            pltpu.VMEM((ROWS, 128), BF16),
            pltpu.VMEM((HEADS, ROWS, 256), F32),
            pltpu.VMEM((ROWS, 128), BF16),
            pltpu.VMEM((HEADS, ROWS, 256), F32),
            pltpu.VMEM((HEADS, ROWS, ROWS), F32),
            pltpu.VMEM((HEADS, ROWS, 128), BF16),
            pltpu.VMEM((HEADS, ROWS, 128), BF16),
            pltpu.VMEM((HEADS, ROWS, 128), BF16),
            pltpu.VMEM((16, 32, 56, 128), BF16),
            pltpu.VMEM((HEADS, WIDTH, 256), BF16),
            pltpu.VMEM((FEATURES, WIDTH), BF16),
            pltpu.VMEM((FEATURES, WIDTH), BF16),
            pltpu.VMEM((HEADS, ROWS, 128), BF16),
            pltpu.VMEM((HEADS, ROWS, 128), F32),
            pltpu.VMEM((HEADS, ROWS, ROWS), F32),
            pltpu.VMEM((HEADS, ROWS, ROWS), BF16),
            pltpu.VMEM((HEADS, ROWS, 128), F32),
            pltpu.VMEM((HEADS, ROWS, 128), F32),
            pltpu.SemaphoreType.DMA((16,)),
        ],
        [HBM] * 7,
        limit=57,
        out_space=pltpu.HBM,
        us=25,
    )(gathered, *operands)


def temporal_grad_kernel(modded, reduced, d_projected, d_reduced, grad, ups):
    ups[:, 1664:] = jnp.zeros((64, 128), F32)
    for head in range(HEADS):
        high, rest = halves(d_projected[head])
        both = dot(reduced[...], jnp.concatenate([high, rest], 1), TN)
        part = both[:64, :256] + both[64:, :256] + both[:64, 256:] + both[64:, 256:]
        for k in range(3):
            begin = k * FEATURES + head * HEAD
            ups[:, begin : begin + HEAD] = part[:, k * HEAD : k * HEAD + HEAD]
    down = dot(d_reduced[...], modded[...], TN)
    store_tiles(grad, 0, down[:64] + down[64:])
    store_tiles(grad, 9, ups[...])


def temporal_grad(*operands):
    return call(
        temporal_grad_kernel,
        jax.ShapeDtypeStruct((RANK, 23, 128), F32),
        [pltpu.VMEM((RANK, 1792), F32)],
    )(*operands)


def epilogue_kernel(place, own, other, grad_down, grad_up):
    for side, ref in enumerate((own, other)):
        core = place[2] if side == 0 else 1 - place[2]
        rows = pl.ds(pl.multiple_of(core * 32, 32), 32)
        for tile in range(9):
            columns = slice(128 * tile, 128 * tile + 128)
            grad_down[0, rows, columns] = ref[:, tile, :]
            grad_down[1, rows, columns] = ref[:, 25 + tile, :]
        for head in range(HEADS):
            both = jnp.concatenate([ref[:, 9 + 2 * head, :], ref[:, 10 + 2 * head, :]], 1)
            for k in range(3):
                start = k * FEATURES + head * HEAD
                grad_up[0, rows, start : start + HEAD] = both[:, k * HEAD : k * HEAD + HEAD]
        for tile in range(13):
            grad_up[1, rows, 128 * tile : 128 * tile + 128] = ref[:, 34 + tile, :]
        grad_up[1, rows, 1664:1728] = ref[:, 47, :][:, :64]


def epilogue(place, own, other):
    vmem = spec(pltpu.VMEM)
    return call(
        epilogue_kernel,
        (
            jax.ShapeDtypeStruct((2, RANK, WIDTH), F32),
            jax.ShapeDtypeStruct((2, RANK, 3 * FEATURES), F32),
        ),
        in_specs=[spec(pltpu.SMEM), vmem, vmem],
    )(place, own, other)


def exchange(values, axes):
    return lax.all_to_all(values, axes, 0, 0)


def spread(values, axes, count):
    return exchange(jnp.broadcast_to(values[None], (count,) + values.shape), axes)


def swap_cores(values):
    return lax.ppermute(values, "c", [(0, 1), (1, 0)])


def add_cores(values, c):
    mine = lax.dynamic_slice_in_dim(values, c * 32, 32, 0)
    return mine, swap_cores(lax.dynamic_slice_in_dim(values, (1 - c) * 32, 32, 0))


def on_device(latents, targets, modulation, qkv, out, down, up):
    x, l, c = lax.axis_index("x"), lax.axis_index("l"), lax.axis_index("c")
    place = jnp.stack([x * 2 + c, l, c]).astype(jnp.int32)
    modulation = modulation[0].transpose(1, 0, 2)
    modded, part, first = prologue(
        place,
        latents[0, 0],
        modulation,
        qkv.transpose(1, 0, 2),
        out.transpose(1, 0, 2),
    )
    modded = lax.all_gather(modded, ("x", "c"), axis=0, tiled=False)
    gathered = lax.all_gather(exchange(part, DP), SEQ, axis=0, tiled=False)
    first = exchange(first, DP)
    down_first, down_second, up_first, up_second = adapters(place, down.transpose(0, 2, 1), up)
    sent, projected, reduced, weights = spatial(
        modded, first, down_first, up_first, latents[0, 0], targets[0, 0]
    )
    received = exchange(sent, SEQ)
    cosine, sine = rotation_tables()
    sent, *saved = temporal(
        gathered,
        received,
        modulation,
        down_second,
        up_second,
        jnp.asarray(cosine),
        jnp.asarray(sine),
    )
    cotangent = exchange(sent, SEQ)
    late = sum(add_cores(temporal_grad(*saved), c))
    early = spatial_back(cotangent, up_first, modded, projected, reduced, weights)
    mine, other = add_cores(early, c)
    first_up, second_up = mine[:, 9:], other[:, 9:]
    total = jnp.concatenate(
        [
            mine[:, :9] + other[:, :9],
            jnp.where(c == 0, first_up, second_up),
            jnp.where(c == 0, second_up, first_up),
            late,
        ],
        1,
    )
    total = exchange(total.reshape(32, 9, 4, 128), ("z", "x")).reshape(32, 36, 128)
    ups = jnp.sum(total[:, 9:13].reshape(8, 4, 4, 128), 0).reshape(16, 128)
    total = jnp.concatenate([jnp.sum(total[:, :9], 0), ups, jnp.sum(total[:, 13:], 0)], 0)
    total = jnp.sum(spread(total, ("h", "l"), 8), 0)
    total = spread(total, ("z", "x"), 32)
    grad_down, grad_up = epilogue(place, total, swap_cores(total))
    return grad_down.transpose(0, 2, 1), grad_up


def solution(mesh):
    inner = Mesh(mesh.devices.reshape(8, 4, 4, 2, 2), ("z", "h", "x", "l", "c"))
    in_specs = (
        P(DP, SEQ, None, None),
        P(DP, SEQ, None, None),
        P(DP, None, None, None),
        P(None, DP, None),
        P(None, DP, None),
        P(),
        P(),
    )
    return jax.shard_map(
        on_device, mesh=inner, in_specs=in_specs, out_specs=(P(), P()), check_vma=False
    )
```
